768 devices in a mesh: shard: 16 (over y, core), rep: 48 (over z, x).
Axes of the slice: x: 4, y: 8, z: 12, core: 2. Of those that a mesh axis runs over, the one named last changes fastest.
Arguments:
- node_feats: bfloat16 [196608, 512], P(('shard', 'rep')), may hold values from -6 to 6
- send_rows: int32 [768, 16, 32], P(('shard', 'rep')), may hold values from 0 to 255
- neighbors: int32 [196608, 16], P(('shard', 'rep')), may hold values from 0 to 767
- neighbor_weight: float32 [196608, 16], P(('shard', 'rep')), may hold values from 0.1 to 1
- gcn_weight: bfloat16 [1024, 512], replicated, may hold values from -0.1875 to 0.1875
- user_dense: bfloat16 [6144, 512], P(('shard', 'rep')), may hold values from -6 to 6
- cand_owner: int32 [6144, 50, 1], P(('shard', 'rep')), may hold values from 0 to 15; in each aligned block of 400 rows (0 to 399, 400 to 799, ..., all dimensions but the last counted through in order) at most 56 rows name the same one
- cand_row: int32 [6144, 50], P(('shard', 'rep')), may hold values from 0 to 255
- mlp_weight: bfloat16 [1787, 1024], replicated, may hold values from -0.125 to 0.125
- out_weight: bfloat16 [1024], replicated, may hold values from -0.1875 to 0.1875
- logit_grad: float32 [6144], P(('shard', 'rep')), may hold values from -384 to 384
Outputs:
- item_embedding: bfloat16 [196608, 512], P(('shard', 'rep'))
- embedding_grad: float32 [196608, 512], P(('shard', 'rep'))
- click_logits: float32 [6144], P(('shard', 'rep'))
- gcn_weight_grad: float32 [1024, 512], replicated
The draws below stay inside these ranges and needn't reach their ends.
Inputs may be any that keep to these rules, and one draw needn't show every extreme that they name: `cand_owner`: among the candidates of one device's 8 requests, no owner is named more than 56 times, a bound that some block reaches.
All inputs are finite; a program needn't handle non-finite values.
Results may differ from the reference program's by a relative error of at most 0.015.
Values may be sent and summed in bfloat16 or wider, within the bound.
A program may use at most 32 MiB of HBM per device.

```python
import math
import jax
import jax.numpy as jnp
import numpy as np
from jax import lax

D = 512
HID = 1024
CAND = 50
DEG = 16
NODE_DEV = 256
REQ_DEV = 8
BND = 32
FEAT = 51
MLP_IN = 1787
CAP = 56
EXT = 768
NODES = 196608
REQUESTS = 6144
N_SHARD = 16
N_REP = 48
DEVICES = 768


def plant(drawn, own_key, smallest, high):
    spot = [jax.random.randint(jax.random.fold_in(own_key, axis), (), 0, length) for axis, length in enumerate(drawn.shape)]
    widest = drawn.shape.index(max(drawn.shape))
    next_to = spot[:widest] + [(spot[widest] + 1) % drawn.shape[widest]] + spot[widest + 1:]
    return drawn.at[tuple(spot)].set(smallest).at[tuple(next_to)].set(high)


def block_levels(key, extent, split, least, largest):
    def one(position, shards_of):
        heights = jax.random.uniform(jax.random.fold_in(jax.random.fold_in(key, 6), position), (shards_of,), jnp.float32, least / len(split), largest / len(split))
        return jnp.repeat(jnp.exp(heights), extent[position] // shards_of).reshape((-1,) + (1,) * (len(extent) - position - 1))

    level = one(*split[0])
    for cut in split[1:]:
        level = level * one(*cut)
    return level


def deal_out(own_key, own, number, rows, count, top, bound, slope):
    ranking = jax.random.permutation(own_key, count)
    packed, common = shares(count, rows * top, bound, slope, True), shares(count, rows * top, bound, slope, False)
    places = jnp.arange(count)

    def named(sizes, rotation):
        used = int((sizes > 0).sum())
        fixed = max(1, used // 4)
        shifted = fixed + (places - fixed + rotation * (used - fixed)) % max(1, count - fixed)
        return jnp.zeros((count,), jnp.int32).at[ranking[jnp.where(places < fixed, places, shifted)]].set(jnp.asarray(sizes, jnp.int32))

    sizes = jnp.where(number % 4 == 0, named(packed, number // 4), named(common, number - number // 4 - 1))
    mixed = jax.random.permutation(jax.random.fold_in(own, 3), count)
    source_of, sink = mixed[0:count // 2 * 2:2], mixed[1:count // 2 * 2:2]
    margin = jnp.minimum(sizes[source_of] - 1, bound - sizes[sink]) // 2
    margin = jnp.where((source_of == ranking[0]) | (sink == ranking[0]) | (sizes[sink] == 0), 0, jnp.maximum(margin, 0))
    shifted = jax.random.randint(jax.random.fold_in(own, 4), (count // 2,), 0, 1 << 20) % (margin + 1)
    sizes = sizes.at[source_of].add(-shifted).at[sink].add(shifted)
    members = jnp.searchsorted(jnp.cumsum(sizes), jnp.arange(rows * top), side="right").astype(jnp.int32)
    table = members.reshape(top, rows).T
    table = table[jax.random.permutation(jax.random.fold_in(own, 1), rows)]
    rotation = jax.random.randint(jax.random.fold_in(own, 2), (rows, 1), 0, top)
    return jnp.take_along_axis(table, (jnp.arange(top)[None, :] + rotation) % top, axis=1)


def shares(count, total, limit, skew, full):
    weights = [(1 << 20) // math.isqrt(rank ** skew) + 1 for rank in range(1, count + 1)]
    largest = limit if full else min(limit, max(-(-total // count), total * weights[0] // sum(weights)))
    least = 1 if total - largest >= count - 1 else 0
    counts, spare = [largest] + [least] * (count - 1), total - largest - least * (count - 1)
    while spare > 0:
        free = [i for i in range(1, count) if counts[i] < largest] or [i for i in range(1, count) if counts[i] < limit]
        whole, remaining = sum([weights[i] for i in free]), spare
        for i in free:
            addition = min(limit - counts[i], max(1, remaining * weights[i] // whole), spare)
            counts[i] = counts[i] + addition
            spare = spare - addition
    return np.array(counts)


def gaussian(key, dims, scale, limit, cuts=(), held_as=jnp.bfloat16):
    entries = scale * jax.random.normal(key, dims, jnp.float32)
    if cuts:
        entries = entries * block_levels(key, dims, cuts, -0.22, 0.18)
    return jnp.clip(entries, -limit, limit).astype(held_as)


def setup_inputs(seed: int = 0) -> dict:
    keys = jax.random.split(jax.random.key(seed), 12)
    node_feats = gaussian(keys[0], (NODES, D), 1.0, 6.0, ((0, 768),))
    send_rows = plant(jax.random.randint(keys[1], (DEVICES, N_SHARD, BND), 0, NODE_DEV), jax.random.fold_in(keys[1], 1), 0, NODE_DEV - 1).astype(jnp.int32)
    neighbors = plant(jax.random.randint(keys[2], (NODES, DEG), 0, EXT), jax.random.fold_in(keys[2], 1), 0, EXT - 1).astype(jnp.int32)
    neighbor_weight = jnp.clip(jnp.exp(math.log(1.0) - 2.3025851 * jax.random.uniform(keys[3], (NODES, DEG), jnp.float32) ** block_levels(keys[3], (NODES, DEG), ((0, 768),), -0.2, 0.2)), 0.1, 1.0)
    gcn_weight = gaussian(keys[4], (2 * D, D), (2 * D) ** -0.5, 0.1875)
    user_dense = gaussian(keys[5], (REQUESTS, D), 1.0, 6.0, ((0, 768),))
    cand_owner_keys = jax.random.split(jax.random.fold_in(keys[6], 1), REQUESTS * CAND // (REQ_DEV * CAND))
    cand_owner_turns = jax.random.permutation(jax.random.fold_in(keys[6], 3), REQUESTS * CAND // (REQ_DEV * CAND))
    cand_owner = jax.vmap(lambda own, number: deal_out(jax.random.fold_in(keys[6], 2), own, number, REQ_DEV * CAND, N_SHARD, 1, CAP, 2))(cand_owner_keys, cand_owner_turns).reshape((REQUESTS, CAND, 1))
    cand_row = plant(jax.random.randint(keys[7], (REQUESTS, CAND), 0, NODE_DEV), jax.random.fold_in(keys[7], 1), 0, NODE_DEV - 1).astype(jnp.int32)
    mlp_weight = gaussian(keys[8], (MLP_IN, HID), MLP_IN ** -0.5, 0.125)
    out_weight = gaussian(keys[9], (HID,), HID ** -0.5, 0.1875)
    logit_grad = gaussian(keys[10], (REQUESTS,), 64.0, 384.0, ((0, 768),), jnp.float32)
    return {"node_feats": node_feats, "send_rows": send_rows, "neighbors": neighbors, "neighbor_weight": neighbor_weight, "gcn_weight": gcn_weight, "user_dense": user_dense, "cand_owner": cand_owner, "cand_row": cand_row, "mlp_weight": mlp_weight, "out_weight": out_weight, "logit_grad": logit_grad}


def pair_tables(count):
    lower_i, lower_j = np.tril_indices(count, -1)
    pair_table = (lower_i * count + lower_j).astype(np.int32)
    sym_table = np.full((count * count,), lower_i.shape[0], dtype=np.int32)
    sym_table[lower_i * count + lower_j] = np.arange(lower_i.shape[0])
    sym_table[lower_j * count + lower_i] = np.arange(lower_i.shape[0])
    return (pair_table, sym_table)

def normalize(projected):
    return projected * lax.rsqrt(lax.optimization_barrier(jnp.mean(projected * projected, axis=-1, keepdims=True)) + 1e-06)

def local_layer(tables, own_rows, indices, weights, gcn_weight):
    picked = tables[indices].astype(jnp.float32)
    summed = lax.optimization_barrier(jnp.sum(weights[:, :, None] * picked, axis=1))
    aggregated = (summed / lax.optimization_barrier(jnp.sum(weights, axis=1))[:, None]).astype(jnp.bfloat16)
    joined = jnp.concatenate([own_rows, aggregated], axis=1)
    projected = jnp.dot(joined, gcn_weight, preferred_element_type=jnp.float32)
    return (joined, projected)

def reference(node_feats, send_rows, neighbors, neighbor_weight, gcn_weight, user_dense, cand_owner, cand_row, mlp_weight, out_weight, logit_grad):
    feat_blocks = node_feats.reshape(N_SHARD, N_REP, NODE_DEV, D)
    send_blocks = send_rows.reshape(N_SHARD, N_REP, N_SHARD * BND)
    sent_rows = jax.vmap(jax.vmap(lambda source, picks: source[picks]))(feat_blocks, send_blocks)
    sent_rows = sent_rows.reshape(N_SHARD, N_REP, N_SHARD, BND, D)
    received = jnp.transpose(sent_rows, (2, 1, 0, 3, 4)).reshape(DEVICES, N_SHARD * BND, D)
    own_rows = node_feats.reshape(DEVICES, NODE_DEV, D)
    tables = jnp.concatenate([own_rows, received], axis=1)
    indices = neighbors.reshape(DEVICES, NODE_DEV, DEG)
    weights = neighbor_weight.reshape(DEVICES, NODE_DEV, DEG)

    def forward_block(pieces):
        joined, projected = local_layer(pieces[0], pieces[1], pieces[2], pieces[3], gcn_weight)
        return normalize(projected).astype(jnp.bfloat16)
    embeddings = lax.map(forward_block, (tables, own_rows, indices, weights))
    emb_blocks = embeddings.reshape(N_SHARD, N_REP, NODE_DEV, D)
    groups = jnp.arange(REQUESTS, dtype=jnp.int32) // REQ_DEV % N_REP
    owners = cand_owner[:, :, 0]
    groups = jnp.broadcast_to(groups[:, None], owners.shape)
    candidates = emb_blocks[owners, groups, cand_row]
    stacked = jnp.concatenate([user_dense[:, None, :], candidates], axis=1)
    stacked_wide = stacked.astype(jnp.float32)
    grams = jnp.einsum('qid,qjd->qij', stacked_wide, stacked_wide) / math.sqrt(D)
    pair_table, sym_table = pair_tables(FEAT)
    lower_part = grams.reshape(REQUESTS, FEAT * FEAT)[:, pair_table]
    mixed = jnp.concatenate([user_dense.astype(jnp.float32), lower_part], axis=1).astype(jnp.bfloat16)
    hidden_pre = jnp.dot(mixed, mlp_weight, preferred_element_type=jnp.float32)
    hidden_act, gelu_back = jax.vjp(jax.nn.gelu, hidden_pre)
    hidden = hidden_act.astype(jnp.bfloat16)
    click_logits = jnp.dot(hidden, out_weight, preferred_element_type=jnp.float32)
    hidden_grad = gelu_back(logit_grad[:, None] * out_weight.astype(jnp.float32)[None, :])[0].astype(jnp.bfloat16)
    mixed_grad = jnp.dot(hidden_grad, mlp_weight.T, preferred_element_type=jnp.float32)
    lower_grad = jnp.concatenate([mixed_grad[:, D:], jnp.zeros((REQUESTS, 1), jnp.float32)], axis=1)
    sym_grad = lower_grad[:, sym_table].reshape(REQUESTS, FEAT, FEAT).astype(jnp.bfloat16)
    stacked_grad = jnp.einsum('qij,qjd->qid', sym_grad.astype(jnp.float32), stacked_wide) / math.sqrt(D)
    cand_grad = stacked_grad[:, 1:].astype(jnp.bfloat16)
    embed_grad = jnp.zeros((N_SHARD, N_REP, NODE_DEV, D), jnp.float32).at[owners, groups, cand_row].add(cand_grad.astype(jnp.float32))
    embed_grad = embed_grad.reshape(DEVICES, NODE_DEV, D)

    def backward_block(running, pieces):
        joined, projected = local_layer(pieces[0], pieces[1], pieces[2], pieces[3], gcn_weight)
        unused, norm_back = jax.vjp(normalize, projected)
        pre_norm_grad = norm_back(pieces[4])[0].astype(jnp.bfloat16)
        return (running + jnp.dot(joined.T, pre_norm_grad, preferred_element_type=jnp.float32), None)
    summed_grad, unused = lax.scan(backward_block, jnp.zeros((2 * D, D), jnp.float32), (tables, own_rows, indices, weights, embed_grad))
    return (embeddings.reshape(NODES, D), embed_grad.reshape(NODES, D), click_logits, summed_grad / DEVICES)
```

```python
import math

import jax
import jax.numpy as jnp
import numpy as np
from jax import lax
from jax.experimental import pallas as pl
from jax.experimental.pallas import tpu as pltpu
from jax.sharding import PartitionSpec as P


CHUNKS = 2
N_CORE, N_X, N_Y, N_Z = 2, 4, 8, 12
MESH = pl.DeviceIdType.MESH


def places():
    shard, rep = lax.axis_index("shard"), lax.axis_index("rep")
    return lax.div(shard, 2), lax.rem(shard, 2), lax.div(rep, 4), lax.rem(rep, 4)


def reduce_kernel(
    part_ref, out_ref, send0, recv0, half, send1, recv1, send2, recv2, slots3, fin4, fin5, fin6, s_sem, r_sem
):
    y, core, z, x = places()
    other_core = {"shard": y * 2 + 1 - core}

    def at_x(k):
        return {"rep": z * 4 + lax.rem(x + k, N_X)}

    def at_y(k):
        return {"shard": lax.rem(y + k, N_Y) * 2 + core}

    def at_z(k):
        return {"rep": lax.rem(z + k, N_Z) * 4 + x}

    peers = [other_core] + [at_x(k) for k in range(1, N_X)]
    peers += [at_y(k) for k in range(1, N_Y)] + [at_z(k) for k in range(1, N_Z)]
    barrier = pltpu.get_barrier_semaphore()
    for peer in peers:
        pl.semaphore_signal(barrier, inc=1, device_id=peer, device_id_type=MESH)
    pl.semaphore_wait(barrier, len(peers))

    rows, width = part_ref.shape
    chunk = width // CHUNKS
    wide = jnp.float32
    thin = jnp.bfloat16
    in_flight = {}

    def send(c, number, src, dst, peer):
        copy = pltpu.make_async_remote_copy(
            src_ref=src,
            dst_ref=dst,
            send_sem=s_sem.at[c, number],
            recv_sem=r_sem.at[c, number],
            device_id=peer,
            device_id_type=MESH,
        )
        copy.start()
        in_flight[c, number] = copy

    def arrive(c, numbers):
        for number in numbers:
            in_flight[c, number].wait()

    def step0(c):
        cols = pl.ds(c * chunk, chunk)
        theirs = pl.multiple_of((1 - core) * (rows // 2), rows // 2)
        send0[c] = part_ref[pl.ds(theirs, rows // 2), cols].astype(thin)
        send(c, 0, send0.at[c], recv0.at[c], other_core)

    def step1(c):
        arrive(c, [0])
        cols = pl.ds(c * chunk, chunk)
        mine = pl.multiple_of(core * (rows // 2), rows // 2)
        total = part_ref[pl.ds(mine, rows // 2), cols] + recv0[c].astype(wide)
        half[c] = total.reshape(N_X, rows // 8, chunk)
        send1[c] = total.astype(thin).reshape(N_X, rows // 8, chunk)
        for k in range(1, N_X):
            to = lax.rem(x + k, N_X)
            send(c, k, send1.at[c, to], recv1.at[c, k - 1], at_x(k))

    def step2(c):
        arrive(c, range(1, 4))
        total = half[c, x]
        for k in range(3):
            total = total + recv1[c, k].astype(wide)
        half[c, 0] = total
        send2[c] = total.astype(thin).reshape(N_Y, rows // 64, chunk)
        for k in range(1, N_Y):
            to = lax.rem(y + k, N_Y)
            send(c, 3 + k, send2.at[c, to], recv2.at[c, k - 1], at_y(k))

    def step3(c):
        arrive(c, range(4, 11))
        total = half[c, 0, pl.ds(pl.multiple_of(y * (rows // 64), rows // 64), rows // 64)]
        for k in range(7):
            total = total + recv2[c, k].astype(wide)
        slots3[c, z] = total.astype(thin)
        for k in range(1, N_Z):
            send(c, 10 + k, slots3.at[c, z], slots3.at[c, z], at_z(k))

    def step4(c):
        arrive(c, range(11, 22))
        total = slots3[c, 0].astype(wide)
        for k in range(1, N_Z):
            total = total + slots3[c, k].astype(wide)
        fin4[c, y] = (total * (1.0 / 768)).astype(thin)
        for k in range(1, N_Y):
            send(c, 21 + k, fin4.at[c, y], fin4.at[c, y], at_y(k))

    def step5(c):
        arrive(c, range(22, 29))
        fin5[c, x] = fin4[c].reshape(rows // 8, chunk)
        for k in range(1, N_X):
            send(c, 28 + k, fin5.at[c, x], fin5.at[c, x], at_x(k))

    def step6(c):
        arrive(c, range(29, 32))
        fin6[c, core] = fin5[c].reshape(rows // 2, chunk)
        send(c, 32, fin6.at[c, core], fin6.at[c, core], other_core)

    def step7(c):
        arrive(c, [32])
        out_ref[:, c * chunk : (c + 1) * chunk] = fin6[c].reshape(rows, chunk)

    steps = (step0, step1, step2, step3, step4, step5, step6, step7)
    for wave in range(len(steps) + CHUNKS - 1):
        for c in range(CHUNKS):
            if 0 <= wave - c < len(steps):
                steps[wave - c](c)


def mean_over_devices(term):
    rows, width = term.shape
    chunk = width // CHUNKS
    thin, wide = jnp.bfloat16, jnp.float32
    eighth, block = rows // 8, rows // 64
    mean = pl.pallas_call(
        reduce_kernel,
        out_shape=jax.ShapeDtypeStruct((rows, width), thin),
        in_specs=[pl.BlockSpec(memory_space=pltpu.VMEM)],
        out_specs=pl.BlockSpec(memory_space=pltpu.VMEM),
        scratch_shapes=[
            pltpu.VMEM((CHUNKS, rows // 2, chunk), thin),
            pltpu.VMEM((CHUNKS, rows // 2, chunk), thin),
            pltpu.VMEM((CHUNKS, N_X, eighth, chunk), wide),
            pltpu.VMEM((CHUNKS, N_X, eighth, chunk), thin),
            pltpu.VMEM((CHUNKS, N_X - 1, eighth, chunk), thin),
            pltpu.VMEM((CHUNKS, N_Y, block, chunk), thin),
            pltpu.VMEM((CHUNKS, N_Y - 1, block, chunk), thin),
            pltpu.VMEM((CHUNKS, N_Z, block, chunk), thin),
            pltpu.VMEM((CHUNKS, N_Y, block, chunk), thin),
            pltpu.VMEM((CHUNKS, N_X, eighth, chunk), thin),
            pltpu.VMEM((CHUNKS, N_CORE, rows // 2, chunk), thin),
            pltpu.SemaphoreType.DMA((CHUNKS, 33)),
            pltpu.SemaphoreType.DMA((CHUNKS, 33)),
        ],
        compiler_params=pltpu.CompilerParams(
            collective_id=0, has_side_effects=True, vmem_limit_bytes=48 * 1024 * 1024
        ),
    )(term)
    return mean.astype(wide)


def pair_tables(count):
    lower_i, lower_j = np.tril_indices(count, -1)
    pair_table = (lower_i * count + lower_j).astype(np.int32)
    sym_table = np.full((count * count,), lower_i.shape[0], dtype=np.int32)
    sym_table[lower_i * count + lower_j] = np.arange(lower_i.shape[0])
    sym_table[lower_j * count + lower_i] = np.arange(lower_i.shape[0])
    return (pair_table, sym_table)


def normalize(projected):
    return projected * lax.rsqrt(jnp.mean(projected * projected, axis=-1, keepdims=True) + 1e-06)


def local_layer(tables, own_rows, indices, weights, gcn_weight):
    picked = tables[indices].astype(jnp.float32)
    summed = jnp.sum(weights[:, :, None] * picked, axis=1)
    aggregated = (summed / jnp.sum(weights, axis=1)[:, None]).astype(jnp.bfloat16)
    joined = jnp.concatenate([own_rows, aggregated], axis=1)
    projected = jnp.dot(joined, gcn_weight, preferred_element_type=jnp.float32)
    return (joined, projected)


def on_device(
    node_feats,
    send_rows,
    neighbors,
    neighbor_weight,
    gcn_weight,
    user_dense,
    cand_owner,
    cand_row,
    mlp_weight,
    out_weight,
    logit_grad,
):
    peer_count = lax.axis_size("shard")
    node_count, model_width = node_feats.shape
    outgoing = node_feats[send_rows[0].reshape(-1)].reshape(peer_count, -1, model_width)
    incoming = lax.all_to_all(outgoing, "shard", split_axis=0, concat_axis=0, tiled=True)
    tables = jnp.concatenate([node_feats, incoming.reshape(-1, model_width)], axis=0)
    joined, projected = local_layer(tables, node_feats, neighbors, neighbor_weight, gcn_weight)
    embeddings = normalize(projected).astype(jnp.bfloat16)
    requests, candidates = cand_row.shape
    capacity = 9 * requests * candidates // (4 * peer_count)
    owners = cand_owner.reshape(-1)
    wanted_rows = cand_row.reshape(-1)
    owner_hits = (owners[:, None] == jnp.arange(peer_count, dtype=jnp.int32)[None, :]).astype(
        jnp.int32
    )
    slot_rank = jnp.sum(jnp.cumsum(owner_hits, axis=0) * owner_hits, axis=1) - 1
    slot_of = owners * capacity + slot_rank
    wanted = (
        jnp.zeros((peer_count * capacity,), jnp.int32)
        .at[slot_of]
        .set(wanted_rows)
        .reshape(peer_count, capacity)
    )
    asked = lax.all_to_all(wanted, "shard", split_axis=0, concat_axis=0, tiled=True)
    looked_up = embeddings[asked]
    returned = lax.all_to_all(looked_up, "shard", split_axis=0, concat_axis=0, tiled=True)
    cand_rows = returned.reshape(peer_count * capacity, model_width)[slot_of].reshape(
        requests, candidates, model_width
    )
    stacked = jnp.concatenate([user_dense[:, None, :], cand_rows], axis=1)
    scale = math.sqrt(model_width)
    grams = jnp.einsum("qid,qjd->qij", stacked, stacked, preferred_element_type=jnp.float32) / scale
    pair_table, sym_table = pair_tables(candidates + 1)
    lower_part = grams.reshape(requests, -1)[:, pair_table]
    mixed = jnp.concatenate([user_dense, lower_part.astype(jnp.bfloat16)], axis=1)
    hidden_pre = jnp.dot(mixed, mlp_weight, preferred_element_type=jnp.float32)
    hidden_act, gelu_back = jax.vjp(jax.nn.gelu, hidden_pre)
    hidden = hidden_act.astype(jnp.bfloat16)
    click_logits = jnp.dot(hidden, out_weight, preferred_element_type=jnp.float32)
    hidden_grad = gelu_back(logit_grad[:, None] * out_weight.astype(jnp.float32)[None, :])[
        0
    ].astype(jnp.bfloat16)
    mixed_grad = lax.dot_general(
        hidden_grad, mlp_weight, (((1,), (1,)), ((), ())), preferred_element_type=jnp.float32
    )
    lower_grad = jnp.concatenate(
        [mixed_grad[:, model_width:], jnp.zeros((requests, 1), jnp.float32)], axis=1
    )
    sym_grad = (
        lower_grad[:, sym_table]
        .reshape(requests, candidates + 1, candidates + 1)
        .astype(jnp.bfloat16)
    )
    stacked_grad = (
        jnp.einsum("qij,qjd->qid", sym_grad, stacked, preferred_element_type=jnp.float32) / scale
    )
    cand_grad = stacked_grad[:, 1:].astype(jnp.bfloat16).reshape(-1, model_width)
    outboxes = (
        jnp.zeros((peer_count * capacity, model_width), jnp.bfloat16).at[slot_of].set(cand_grad)
    )
    inboxes = lax.all_to_all(
        outboxes.reshape(peer_count, capacity, model_width),
        "shard",
        split_axis=0,
        concat_axis=0,
        tiled=True,
    )
    embed_grad = (
        jnp.zeros((node_count, model_width), jnp.float32)
        .at[asked.reshape(-1)]
        .add(inboxes.reshape(-1, model_width).astype(jnp.float32))
    )
    unused, norm_back = jax.vjp(normalize, projected)
    pre_norm_grad = norm_back(embed_grad)[0].astype(jnp.bfloat16)
    grad_term = lax.dot_general(
        joined, pre_norm_grad, (((0,), (0,)), ((), ())), preferred_element_type=jnp.float32
    )
    gcn_weight_grad = mean_over_devices(grad_term)
    return (embeddings, embed_grad, click_logits, gcn_weight_grad)


def solution(mesh):
    return jax.shard_map(
        on_device,
        mesh=mesh,
        in_specs=(
            P(("shard", "rep"), None),
            P(("shard", "rep"), None, None),
            P(("shard", "rep"), None),
            P(("shard", "rep"), None),
            P(),
            P(("shard", "rep"), None),
            P(("shard", "rep"), None, None),
            P(("shard", "rep"), None),
            P(),
            P(),
            P(("shard", "rep")),
        ),
        out_specs=(P(("shard", "rep"), None), P(("shard", "rep"), None), P(("shard", "rep")), P()),
        check_vma=False,
    )
```

```python
import math

import jax
import jax.numpy as jnp
from jax import lax
from jax.experimental import pallas as pl
from jax.experimental.pallas import tpu as pltpu
from jax.sharding import PartitionSpec as P

MESH = pl.DeviceIdType.MESH
F32, BF16, I32, I16 = jnp.float32, jnp.bfloat16, jnp.int32, jnp.int16
N_X, N_Y, N_Z, GROUP = 4, 8, 12, 16
NODES, WIDTH, DEG, BND = 256, 512, 16, 32
REQS, CAND, PAD, CAP = 8, 50, 64, 56
SLOTS = REQS * PAD
PAIRS = CAND * (CAND + 1) // 2
CHUNKS = 2
ROOT = 1.0 / math.sqrt(WIDTH)


def mm(a, b):
    return lax.dot_general(a, b, (((1,), (0,)), ((), ())), preferred_element_type=F32)


def nt(a, b):
    return lax.dot_general(a, b, (((1,), (1,)), ((), ())), preferred_element_type=F32)


def tn(a, b):
    return lax.dot_general(a, b, (((0,), (0,)), ((), ())), preferred_element_type=F32)


def iota(shape, axis):
    return lax.broadcasted_iota(I32, shape, axis)


def mark(condition):
    return jnp.where(condition, 1.0, 0.0).astype(BF16)


def rows_at(start, count, unit):
    return pl.ds(pl.multiple_of(start, unit), count)


def wide(column, times):
    return jnp.concatenate([column] * times, axis=1)


def kernel(
    feats,
    send_rows,
    neighbors,
    weights,
    gcn_hbm,
    user,
    owners,
    wanted,
    mlp_hbm,
    out_weight,
    logit_grad,
    emb_out,
    grad_out,
    click_out,
    mean_out,
    meta,
    table,
    owner_b,
    row_b,
    place,
    msg_out,
    msg_in,
    cid,
    gid,
    wgt,
    wsum,
    picks,
    mix,
    halo_pick,
    halo,
    own_id,
    own_w,
    own_mix,
    acc,
    joined,
    unit,
    inv,
    stack,
    grams,
    lower,
    pair_grad,
    cand_grad,
    pre_grad,
    term,
    outbox,
    inbox,
    spread,
    mlp,
    gcn,
    send0,
    recv0,
    half,
    send1,
    recv1,
    send2,
    recv2,
    slots3,
    fin4,
    fin5,
    fin6,
    w_sem,
    meta_s,
    meta_r,
    metac_s,
    metac_r,
    feat_s,
    feat_r,
    featc_s,
    featc_r,
    msg_s,
    msg_r,
    box_s,
    box_r,
    red_s,
    red_r,
):
    shard, rep = lax.axis_index("shard"), lax.axis_index("rep")
    y, core = lax.div(shard, 2), lax.rem(shard, 2)
    z, x = lax.div(rep, N_X), lax.rem(rep, N_X)
    me = shard

    def at_shard(k):
        return {"shard": lax.rem(shard + k, GROUP)}

    def at_x(k):
        return {"rep": z * N_X + lax.rem(x + k, N_X)}

    def at_y(k):
        return {"shard": lax.rem(y + k, N_Y) * 2 + core}

    def at_z(k):
        return {"rep": lax.rem(z + k, N_Z) * N_X + x}

    other_core = {"shard": y * 2 + 1 - core}
    right, left = at_y(1), at_y(N_Y - 1)

    peers = [at_shard(k) for k in range(1, GROUP)]
    peers += [at_x(k) for k in range(1, N_X)] + [at_z(k) for k in range(1, N_Z)]
    barrier = pltpu.get_barrier_semaphore()
    for peer in peers:
        pl.semaphore_signal(barrier, inc=1, device_id=peer, device_id_type=MESH)

    local = [
        pltpu.make_async_copy(gcn_hbm, gcn, w_sem.at[0]),
        pltpu.make_async_copy(mlp_hbm, mlp, w_sem.at[1]),
    ]
    for copy in local:
        copy.start()

    sent = []

    def send(src, dst, s_sem, r_sem, peer):
        copy = pltpu.make_async_remote_copy(
            src_ref=src,
            dst_ref=dst,
            send_sem=s_sem,
            recv_sem=r_sem,
            device_id=peer,
            device_id_type=MESH,
        )
        copy.start()
        sent.append(copy)
        return copy

    ids = neighbors[...]
    id_hi = lax.shift_right_logical(ids, 8).astype(F32).astype(BF16)
    id_lo = jnp.bitwise_and(ids, 255).astype(F32).astype(BF16)
    w_own = weights[...].astype(BF16)

    def put(values, offset):
        return mm(values, mark(iota((DEG, 128), 1) == iota((DEG, 128), 0) + offset))

    packed = jnp.zeros((128, 128), F32)
    for part in range(2):
        cut = slice(part * 128, part * 128 + 128)
        base = part * 64
        packed = packed + put(id_hi[cut], base) + put(id_lo[cut], base + 16) + put(w_own[cut], base + 32)
    meta[me, 0:128, :] = packed.astype(BF16)
    sr = send_rows[0].astype(F32).astype(BF16)
    meta[me, 128:144, :] = mm(sr, mark(iota((BND, 128), 1) == iota((BND, 128), 0))).astype(BF16)
    table[y, rows_at(core * NODES, NODES, NODES), :] = feats[...]

    pl.semaphore_wait(barrier, len(peers))

    def chip(d):
        return lax.rem(y + d + N_Y, N_Y)

    meta_got, metac_got, feat_got, featc_got = {}, {}, {}, {}

    def meta_ring(way, hop):
        block = chip(-hop if way == 0 else hop) * 2 + core
        ref = meta.at[block]
        number = way * 4 + hop
        meta_got[way, hop] = send(
            ref, ref, meta_s.at[number], meta_r.at[number], right if way == 0 else left
        )

    def meta_core(d, number):
        ref = meta.at[chip(d) * 2 + core]
        metac_got[d] = send(ref, ref, metac_s.at[number], metac_r.at[number], other_core)

    def feat_ref(d, part):
        return table.at[chip(d), rows_at(core * NODES + part * 128, 128, 128)]

    def feat_ring(way, hop, part):
        ref = feat_ref(-hop if way == 0 else hop, part)
        number = (way * 4 + hop) * 2 + part
        feat_got[way, hop, part] = send(
            ref, ref, feat_s.at[number], feat_r.at[number], right if way == 0 else left
        )

    core_order = (0, -1, 1, -2, 2, -3, 3, 4)

    def feat_core(d, part):
        number = core_order.index(d) * 2 + part
        ref = feat_ref(d, part)
        featc_got[d, part] = send(ref, ref, featc_s.at[number], featc_r.at[number], other_core)

    def meta_step(hop):
        meta_got[0, hop].wait_recv()
        if hop < 3:
            meta_ring(0, hop + 1)
            meta_got[1, hop].wait_recv()
            if hop < 2:
                meta_ring(1, hop + 1)
            meta_core(-1 - hop, 1 + 2 * hop)
            meta_core(1 + hop, 2 + 2 * hop)
        else:
            meta_core(4, 7)

    def feat_step(hop, part):
        if hop < 3:
            feat_got[0, hop, part].wait_recv()
            if hop < 2 or part == 0:
                feat_ring(0, hop + 1, part)
            feat_got[1, hop, part].wait_recv()
            if hop < 2 or part == 1:
                feat_ring(1, hop + 1, part)
            feat_core(-1 - hop, part)
            feat_core(1 + hop, part)
        else:
            feat_got[part, hop, part].wait_recv()
            feat_core(4, part)

    meta_ring(0, 0)
    meta_ring(1, 0)
    meta_core(0, 0)
    for part in range(2):
        feat_ring(0, 0, part)
        feat_ring(1, 0, part)
    for part in range(2):
        feat_core(0, part)

    request = lax.shift_right_logical(iota((SLOTS, REQS), 0), 6)
    of_request = mark(request == iota((SLOTS, REQS), 1))
    within = jnp.bitwise_and(iota((SLOTS, CAND), 0), PAD - 1)
    hit = iota((SLOTS, CAND), 1) == within - 1
    spot = jnp.bitwise_and(iota((SLOTS, 128), 0), PAD - 1)
    valid = (spot >= 1) & (spot <= CAND)

    def column(values):
        spread_out = mm(of_request, values.astype(F32).astype(BF16))
        return mm(jnp.where(hit, spread_out, 0.0).astype(BF16), jnp.ones((CAND, 128), BF16))

    owner_col = jnp.where(valid, column(owners[...]), -1.0)
    row_col = jnp.where(valid, column(wanted[...]), 0.0)
    owner_b[...] = owner_col
    row_b[...] = row_col
    cid[...] = jnp.where(valid, owner_col * NODES + row_col, -1.0).astype(I32).astype(I16)

    meta_step(0)

    lanes = iota((SLOTS, 128), 1).astype(F32)
    hits = mark(owner_col == lanes)
    below = mark(iota((SLOTS, SLOTS), 0) >= iota((SLOTS, SLOTS), 1))
    counts = mm(below, hits)
    rank = mm((jnp.where(owner_col == lanes, counts, 0.0)).astype(BF16), jnp.ones((128, 128), BF16))
    slot_col = jnp.where(valid, owner_col * 128 + rank - 1.0, -4096.0)
    slot_lane = slot_col.T[0:16, :]
    row_lane = row_col.T[0:16, :].astype(BF16)

    meta_step(1)

    def place_owner(owner, carry):
        mine = slot_lane[0:1, :] - owner.astype(F32) * 128
        at = iota((128, SLOTS), 0)
        at = jnp.where(at >= CAP, at - CAP, at)
        at = jnp.where(iota((128, SLOTS), 0) >= 2 * CAP, -30000, at)
        chosen = mark(at.astype(F32) == mine)
        place[owner] = chosen
        msg_out[owner] = nt(row_lane, chosen).astype(BF16)
        return carry

    lax.fori_loop(0, GROUP, place_owner, 0)
    meta_step(2)
    msg_in[me] = msg_out[me]
    msg_got = []
    for k in range(1, GROUP):
        to = lax.rem(me + k, GROUP)
        msg_got.append(send(msg_out.at[to], msg_in.at[me], msg_s.at[k - 1], msg_r.at[k - 1], at_shard(k)))
    feat_step(0, 0)

    w_own_sum = mm(w_own, jnp.ones((DEG, 128), BF16))

    def own_k(k, carry):
        pick = mark(iota((DEG, 128), 0) == k)
        own_id[k] = (mm(id_hi, pick) * 256 + mm(id_lo, pick)).astype(I32).astype(I16)
        own_w[k] = mm(w_own, pick).astype(BF16)
        return carry

    lax.fori_loop(0, DEG, own_k, 0)

    def own_rows(tile, carry):
        rows = rows_at(tile * 16, 16, 16)
        found = [own_id[k, rows, :] for k in range(DEG)]
        share = [own_w[k, rows, :] for k in range(DEG)]
        for t in range(6):
            lane = (iota((16, 128), 1) + t * 128).astype(I16)
            total = jnp.zeros((16, 128), BF16)
            for k in range(DEG):
                total = total + jnp.where(found[k] == lane, share[k], jnp.zeros((16, 128), BF16))
            own_mix[rows, t * 128 : t * 128 + 128] = total
        return carry

    lax.fori_loop(0, NODES // 16, own_rows, 0)

    meta_step(3)
    for d in core_order:
        metac_got[d].wait_recv()
    feat_step(0, 1)

    narrow = jnp.where(row_b[...] >= 128, row_b[...] - 128, row_b[...])
    meta_id = jnp.where(valid, owner_b[...] * 128 + narrow, -1.0)

    def meta_pick(p, total):
        chosen = mark(meta_id == (iota((SLOTS, 128), 1) + p * 128).astype(F32))
        return total + mm(chosen, meta[p, 0:128, :])

    got = lax.fori_loop(0, GROUP, meta_pick, jnp.zeros((SLOTS, 128), F32))
    got = jnp.where(row_b[...] >= 128, pltpu.roll(got, 64, 1), got)
    lane128 = iota((SLOTS, 128), 1)
    got = jnp.where(lane128 < 48, got, 0.0).astype(BF16)
    wsum[...] = mm(got, mark(iota((128, 128), 0) >= 32))

    owner16 = mark(owner_b[:, 0:GROUP] == iota((SLOTS, GROUP), 1).astype(F32))
    mine16 = mark(iota((GROUP, 128), 0) == me)
    for j in range(4):
        tile = jnp.zeros((GROUP, 128), F32)
        for i in range(4):
            rows = meta[4 * j + i, 128:144, :].astype(F32)
            tile = tile + (pltpu.roll(rows, 32 * i, 1) if i else rows)
        tile = tile.astype(BF16)
        picks[:, j * 128 : j * 128 + 128] = mm(owner16, tile).astype(BF16)
        from_me = tn(tile, mine16)
        odd = jnp.bitwise_and(lax.shift_right_logical(iota((128, 128), 0), 5), 1).astype(F32)
        from_me = from_me + odd * NODES
        for t in range(4):
            lane = (iota((128, 128), 1) + t * 128).astype(F32)
            halo_pick[j * 128 : j * 128 + 128, t * 128 : t * 128 + 128] = mark(from_me == lane)

    def cand_k(k, carry):
        spots = iota((128, 128), 0)
        hi = mm(got, mark(spots == k))
        lo = mm(got, mark(spots == k + 16))
        wgt[k] = mm(got, mark(spots == k + 32)).astype(BF16)
        ext = hi * 256 + lo - 256
        ext16 = ext.astype(I32).astype(I16)
        found = jnp.zeros((SLOTS, 128), BF16)
        for j in range(4):
            lane = (iota((SLOTS, 128), 1) + j * 128).astype(I16)
            found = found + jnp.where(
                ext16 == lane, picks[:, j * 128 : j * 128 + 128], jnp.zeros((SLOTS, 128), BF16)
            )
        far = mm(found, jnp.ones((128, 128), BF16))
        source = jnp.floor(ext * (1.0 / BND))
        where = jnp.where(hi < 0.5, owner_b[...] * NODES + lo, source * NODES + far)
        gid[k] = where.astype(I32).astype(I16)
        return carry

    lax.fori_loop(0, DEG, cand_k, 0)
    feat_step(1, 0)

    def build(d):
        block = chip(d)

        def rows_of(tile, carry):
            rows = rows_at(tile * 16, 16, 16)
            found = [gid[k, rows, :] for k in range(DEG)]
            share = [wgt[k, rows, :] for k in range(DEG)]
            itself = cid[rows, :]
            nothing = jnp.zeros((16, 128), BF16)
            for t in range(4):
                lane = (iota((16, 128), 1) + (block * 512 + t * 128)).astype(I16)
                cols = slice(t * 128, t * 128 + 128)
                total = nothing
                for k in range(DEG):
                    total = total + jnp.where(found[k] == lane, share[k], nothing)
                mix[block, rows, cols] = jnp.where(itself == lane, jnp.ones((16, 128), BF16), nothing)
                mix[block, rows_at(SLOTS + tile * 16, 16, 16), cols] = total
            return carry

        lax.fori_loop(0, SLOTS // 16, rows_of, 0)

    def absorb(d, first=False):
        block = chip(d)
        for part in range(2):
            featc_got[d, part].wait_recv()

        def rows_of(tile, carry):
            rows = rows_at(tile * 256, 256, 256)
            product = mm(mix[block, rows, :], table[block])
            acc[rows, :] = product if first else acc[rows, :] + product
            return carry

        lax.fori_loop(0, 2 * SLOTS // 256, rows_of, 0)
        pick = rows_at(block * 64, 64, 64)
        halo[pick, :] = mm(halo_pick[pick, :], table[block]).astype(BF16)

    build(0)
    absorb(0, True)
    feat_step(1, 1)
    build(-1)
    absorb(-1)
    build(1)
    absorb(1)
    feat_step(2, 0)
    build(-2)
    build(2)
    feat_step(2, 1)
    absorb(-2)
    absorb(2)
    build(-3)
    build(3)
    build(4)
    feat_step(3, 0)
    feat_step(3, 1)
    absorb(-3)
    absorb(3)
    absorb(4)

    local[0].wait()

    def embed(tile, carry):
        rows = rows_at(tile * 256, 256, 256)
        sums = wsum[rows, :]
        scale = 1.0 / jnp.where(sums > 0, sums, 1.0)
        itself = acc[rows, :].astype(BF16)
        around = (acc[rows_at(SLOTS + tile * 256, 256, 256), :] * wide(scale, 4)).astype(BF16)
        joined[rows, 0:WIDTH] = itself
        joined[rows, WIDTH:] = around
        projected = mm(itself, gcn[0:WIDTH, :]) + mm(around, gcn[WIDTH:, :])
        root = lax.rsqrt(jnp.mean(projected * projected, axis=-1, keepdims=True) + 1e-06)
        ready = projected * root
        unit[rows, :] = ready
        inv[rows, :] = jnp.broadcast_to(root, (256, 128))
        line = iota((256, REQS), 0) + tile * 256
        users = mm(mark(lax.shift_right_logical(line, 6) == iota((256, REQS), 1)), user[...])
        is_user = jnp.bitwise_and(iota((256, WIDTH), 0), PAD - 1) == 0
        stack[rows, :] = jnp.where(is_user, users, ready).astype(BF16)
        return carry

    lax.fori_loop(0, SLOTS // 256, embed, 0)
    stack[SLOTS : SLOTS + PAD, :] = jnp.zeros((PAD, WIDTH), BF16)

    def gram(q, carry):
        grams[q] = nt(stack[rows_at(q * PAD, PAD, PAD), :], stack[rows_at(q * PAD, 2 * PAD, PAD), :]) * ROOT
        return carry

    lax.fori_loop(0, REQS, gram, 0)

    lane8 = iota((REQS, 128), 1)
    strips = [jnp.zeros((REQS, 128), F32) for _ in range(PAIRS // 128 + 2)]
    for i in range(1, CAND + 1):
        strip, shift = divmod(i * (i - 1) // 2, 128)
        line = jnp.where(lane8 < i, grams[:, i, :], 0.0)
        if shift:
            line = pltpu.roll(line, shift, 1)
        if shift + i > 128:
            strips[strip] = strips[strip] + jnp.where(lane8 >= shift, line, 0.0)
            strips[strip + 1] = strips[strip + 1] + jnp.where(lane8 < shift, line, 0.0)
        else:
            strips[strip] = strips[strip] + line
    whole = PAIRS // 128 * 128
    pairs = jnp.concatenate(strips[: PAIRS // 128], axis=1).astype(BF16)
    tail = strips[PAIRS // 128][:, 0 : PAIRS - whole].astype(BF16)

    local[1].wait()
    split = WIDTH + whole
    pre = mm(user[...], mlp[0:WIDTH, :]) + mm(pairs, mlp[WIDTH:split, :])
    pre = pre + mm(tail, mlp[split : WIDTH + PAIRS, :])
    bend = math.sqrt(2.0 / math.pi)
    curve = jnp.tanh(bend * (pre + 0.044715 * (pre * pre * pre)))
    hidden = (pre * (0.5 * (1.0 + curve))).astype(BF16).astype(F32)
    out_w = out_weight[...].astype(F32)
    click = jnp.sum(hidden * out_w, axis=1, keepdims=True)
    click_out[...] = jnp.broadcast_to(click, (REQS, 128))
    slope = 0.5 * (1.0 + curve) + 0.5 * pre * (1.0 - curve * curve) * bend * (1.0 + 3 * 0.044715 * pre * pre)
    hidden_grad = (logit_grad[...] * out_w * slope).astype(BF16)
    pair_grad[:, whole:] = jnp.zeros((REQS, 128), F32)
    pair_grad[:, 0:whole] = nt(hidden_grad, mlp[WIDTH:split, :])
    pair_grad[:, whole:PAIRS] = nt(hidden_grad, mlp[split : WIDTH + PAIRS, :])

    lower[...] = jnp.zeros((REQS, PAD, 128), F32)
    for i in range(1, CAND + 1):
        strip, shift = divmod(i * (i - 1) // 2, 128)
        line = pair_grad[:, strip * 128 : strip * 128 + 128]
        if shift:
            line = pltpu.roll(line, 128 - shift, 1)
        if shift + i > 128:
            more = pltpu.roll(pair_grad[:, strip * 128 + 128 : strip * 128 + 256], 128 - shift, 1)
            line = jnp.where(lane8 < 128 - shift, line, more)
        lower[:, i, :] = jnp.where(lane8 < i, line, 0.0)

    def back(q, carry):
        under = lower[q]
        both = (under[:, 0:PAD] + under.T[0:PAD, :]).astype(BF16)
        rows = rows_at(q * PAD, PAD, PAD)
        grad = mm(both, stack[rows, :]) * ROOT
        row = iota((PAD, WIDTH), 0)
        grad = jnp.where((row >= 1) & (row <= CAND), grad, 0.0).astype(BF16)
        cand_grad[rows, :] = grad
        ready, given = unit[rows, :], grad.astype(F32)
        along = jnp.mean(ready * given, axis=-1, keepdims=True)
        pre_grad[rows, :] = (wide(inv[rows, :], 4) * (given - ready * along)).astype(BF16)
        return carry

    lax.fori_loop(0, REQS, back, 0)

    def weight_term(tile, carry):
        cols = rows_at(tile * 256, 256, 256)
        term[cols, :] = tn(joined[:, cols], pre_grad[...])
        return carry

    lax.fori_loop(0, 4, weight_term, 0)

    rows, width = term.shape
    chunk = width // CHUNKS
    in_flight = {}

    def pass_on(c, number, src, dst, peer):
        in_flight[c, number] = send(src, dst, red_s.at[c, number], red_r.at[c, number], peer)

    def arrive(c, numbers):
        for number in numbers:
            in_flight[c, number].wait_recv()

    def step0(c):
        theirs = pl.multiple_of((1 - core) * (rows // 2), rows // 2)
        send0[c] = term[pl.ds(theirs, rows // 2), c * chunk : (c + 1) * chunk].astype(BF16)
        pass_on(c, 0, send0.at[c], recv0.at[c], other_core)

    def step1(c):
        arrive(c, [0])
        mine = pl.multiple_of(core * (rows // 2), rows // 2)
        total = term[pl.ds(mine, rows // 2), c * chunk : (c + 1) * chunk] + recv0[c].astype(F32)
        half[c] = total.reshape(N_X, rows // 8, chunk)
        send1[c] = total.astype(BF16).reshape(N_X, rows // 8, chunk)
        for k in range(1, N_X):
            to = lax.rem(x + k, N_X)
            pass_on(c, k, send1.at[c, to], recv1.at[c, k - 1], at_x(k))

    def step2(c):
        arrive(c, range(1, 4))
        total = half[c, x]
        for k in range(N_X - 1):
            total = total + recv1[c, k].astype(F32)
        half[c, 0] = total
        send2[c] = total.astype(BF16).reshape(N_Y, rows // 64, chunk)
        for k in range(1, N_Y):
            to = lax.rem(y + k, N_Y)
            pass_on(c, 3 + k, send2.at[c, to], recv2.at[c, k - 1], at_y(k))

    def step3(c):
        arrive(c, range(4, 11))
        total = half[c, 0, rows_at(y * (rows // 64), rows // 64, rows // 64)]
        for k in range(N_Y - 1):
            total = total + recv2[c, k].astype(F32)
        slots3[c, z] = total.astype(BF16)
        for k in range(1, N_Z):
            pass_on(c, 10 + k, slots3.at[c, z], slots3.at[c, z], at_z(k))

    def step4(c):
        arrive(c, range(11, 22))
        total = slots3[c, 0].astype(F32)
        for k in range(1, N_Z):
            total = total + slots3[c, k].astype(F32)
        fin4[c, y] = (total * (1.0 / (GROUP * N_X * N_Z))).astype(BF16)
        for k in range(1, N_Y):
            pass_on(c, 21 + k, fin4.at[c, y], fin4.at[c, y], at_y(k))

    def step5(c):
        arrive(c, range(22, 29))
        fin5[c, x] = fin4[c].reshape(rows // 8, chunk)
        for k in range(1, N_X):
            pass_on(c, 28 + k, fin5.at[c, x], fin5.at[c, x], at_x(k))

    def step6(c):
        arrive(c, range(29, 32))
        fin6[c, core] = fin5[c].reshape(rows // 2, chunk)
        pass_on(c, 32, fin6.at[c, core], fin6.at[c, core], other_core)

    def step7(c):
        arrive(c, [32])
        mean_out[:, c * chunk : (c + 1) * chunk] = fin6[c].reshape(rows, chunk)

    steps = (step0, step1, step2, step3, step4, step5, step6, step7)
    waves = [
        [(wave - c, c) for c in range(CHUNKS) if 0 <= wave - c < len(steps)]
        for wave in range(len(steps) + CHUNKS - 1)
    ]

    def run(wave):
        for step, c in waves[wave]:
            steps[step](c)

    run(0)

    def fill(four, carry):
        chosen = jnp.concatenate([place[four * 4 + j, 0:64, :] for j in range(4)], axis=0)
        picked = mm(chosen, cand_grad[...])
        for j in range(4):
            one = picked[j * 64 : j * 64 + CAP]
            both = jnp.concatenate([one[:, 0 : WIDTH // 2], one[:, WIDTH // 2 :]], axis=0)
            outbox[four * 4 + j] = both.astype(BF16)
        return carry

    lax.fori_loop(0, 4, fill, 0)
    my_box = inbox.at[rows_at(me * 2 * CAP, 2 * CAP, 16)]
    kept = pltpu.make_async_copy(outbox.at[me], my_box, w_sem.at[2])
    kept.start()
    run(1)
    box_got = []
    for k in range(1, GROUP):
        to = lax.rem(me + k, GROUP)
        box_got.append(send(outbox.at[to], my_box, box_s.at[k - 1], box_r.at[k - 1], at_shard(k)))

    shares = mm(own_mix[:, 0:NODES], feats[...]) + mm(own_mix[:, NODES:], halo[...])
    around = (shares * wide(1.0 / w_own_sum, 4)).astype(BF16)
    projected = mm(feats[...], gcn[0:WIDTH, :]) + mm(around, gcn[WIDTH:, :])
    root = lax.rsqrt(jnp.mean(projected * projected, axis=-1, keepdims=True) + 1e-06)
    emb_out[...] = (projected * root).astype(BF16)
    run(2)

    for copy in msg_got:
        copy.wait_recv()
    box_rows = GROUP * 2 * CAP
    lane16 = iota((16, 128), 1)
    marks = [jnp.zeros((16, 128), F32) for _ in range(box_rows // 128 + 1)]
    for p in range(GROUP):
        strip, shift = divmod(p * 2 * CAP, 128)
        line = jnp.where(lane16 < 2 * CAP, msg_in[p].astype(F32), 0.0)
        if shift:
            line = pltpu.roll(line, shift, 1)
        if shift + 2 * CAP > 128:
            marks[strip] = marks[strip] + jnp.where(lane16 >= shift, line, 0.0)
            marks[strip + 1] = marks[strip + 1] + jnp.where(lane16 < shift, line, 0.0)
        else:
            marks[strip] = marks[strip] + line
    run(3)
    for strip in range(box_rows // 128):
        line = lax.rem(iota((1, 128), 1) + strip * 128, 2 * CAP)
        goal = marks[strip][0:1, :]
        cols = slice(strip * 128, strip * 128 + 128)
        here = iota((NODES, 128), 0).astype(F32)
        spread[0:NODES, cols] = mark(here == jnp.where(line < CAP, goal, -1.0))
        spread[NODES:, cols] = mark(here == jnp.where(line < CAP, -1.0, goal))
    for wave in range(4, len(waves)):
        run(wave)

    for copy in box_got:
        copy.wait_recv()
    kept.wait()
    for part in range(2):
        cols = slice(part * NODES, part * NODES + NODES)
        grad_out[:, cols] = mm(spread[cols, :], inbox[...])
    for copy in sent:
        copy.wait_send()


def on_device(
    node_feats,
    send_rows,
    neighbors,
    neighbor_weight,
    gcn_weight,
    user_dense,
    cand_owner,
    cand_row,
    mlp_weight,
    out_weight,
    logit_grad,
):
    rows, width = gcn_weight.shape
    chunk = width // CHUNKS
    eighth, block = rows // 8, rows // 64
    vmem = pl.BlockSpec(memory_space=pltpu.VMEM)
    hbm = pl.BlockSpec(memory_space=pl.ANY)
    dma = pltpu.SemaphoreType.DMA
    embeddings, embed_grad, clicks, mean = pl.pallas_call(
        kernel,
        out_shape=(
            jax.ShapeDtypeStruct((NODES, WIDTH), BF16),
            jax.ShapeDtypeStruct((NODES, WIDTH), F32),
            jax.ShapeDtypeStruct((REQS, 128), F32),
            jax.ShapeDtypeStruct((rows, width), BF16),
        ),
        in_specs=[vmem, vmem, vmem, vmem, hbm, vmem, vmem, vmem, hbm, vmem, vmem],
        out_specs=(vmem, vmem, vmem, vmem),
        scratch_shapes=[
            pltpu.VMEM((GROUP, 144, 128), BF16),
            pltpu.VMEM((N_Y, 2 * NODES, WIDTH), BF16),
            pltpu.VMEM((SLOTS, 128), F32),
            pltpu.VMEM((SLOTS, 128), F32),
            pltpu.VMEM((GROUP, 128, SLOTS), BF16),
            pltpu.VMEM((GROUP, 16, 128), BF16),
            pltpu.VMEM((GROUP, 16, 128), BF16),
            pltpu.VMEM((SLOTS, 128), I16),
            pltpu.VMEM((DEG, SLOTS, 128), I16),
            pltpu.VMEM((DEG, SLOTS, 128), BF16),
            pltpu.VMEM((SLOTS, 128), F32),
            pltpu.VMEM((SLOTS, GROUP * BND), BF16),
            pltpu.VMEM((N_Y, 2 * SLOTS, 2 * NODES), BF16),
            pltpu.VMEM((GROUP * BND, 2 * NODES), BF16),
            pltpu.VMEM((GROUP * BND, WIDTH), BF16),
            pltpu.VMEM((DEG, NODES, 128), I16),
            pltpu.VMEM((DEG, NODES, 128), BF16),
            pltpu.VMEM((NODES, NODES + GROUP * BND), BF16),
            pltpu.VMEM((2 * SLOTS, WIDTH), F32),
            pltpu.VMEM((SLOTS, 2 * WIDTH), BF16),
            pltpu.VMEM((SLOTS, WIDTH), F32),
            pltpu.VMEM((SLOTS, 128), F32),
            pltpu.VMEM((SLOTS + PAD, WIDTH), BF16),
            pltpu.VMEM((REQS, PAD, 128), F32),
            pltpu.VMEM((REQS, PAD, 128), F32),
            pltpu.VMEM((REQS, PAIRS // 128 * 128 + 128), F32),
            pltpu.VMEM((SLOTS, WIDTH), BF16),
            pltpu.VMEM((SLOTS, WIDTH), BF16),
            pltpu.VMEM((rows, width), F32),
            pltpu.VMEM((GROUP, 2 * CAP, WIDTH // 2), BF16),
            pltpu.VMEM((GROUP * 2 * CAP, WIDTH // 2), BF16),
            pltpu.VMEM((2 * NODES, GROUP * 2 * CAP), BF16),
            pltpu.VMEM(mlp_weight.shape, BF16),
            pltpu.VMEM((rows, width), BF16),
            pltpu.VMEM((CHUNKS, rows // 2, chunk), BF16),
            pltpu.VMEM((CHUNKS, rows // 2, chunk), BF16),
            pltpu.VMEM((CHUNKS, N_X, eighth, chunk), F32),
            pltpu.VMEM((CHUNKS, N_X, eighth, chunk), BF16),
            pltpu.VMEM((CHUNKS, N_X - 1, eighth, chunk), BF16),
            pltpu.VMEM((CHUNKS, N_Y, block, chunk), BF16),
            pltpu.VMEM((CHUNKS, N_Y - 1, block, chunk), BF16),
            pltpu.VMEM((CHUNKS, N_Z, block, chunk), BF16),
            pltpu.VMEM((CHUNKS, N_Y, block, chunk), BF16),
            pltpu.VMEM((CHUNKS, N_X, eighth, chunk), BF16),
            pltpu.VMEM((CHUNKS, 2, rows // 2, chunk), BF16),
            dma((3,)),
            dma((8,)),
            dma((8,)),
            dma((8,)),
            dma((8,)),
            dma((16,)),
            dma((16,)),
            dma((16,)),
            dma((16,)),
            dma((GROUP - 1,)),
            dma((GROUP - 1,)),
            dma((GROUP - 1,)),
            dma((GROUP - 1,)),
            dma((CHUNKS, 33)),
            dma((CHUNKS, 33)),
        ],
        compiler_params=pltpu.CompilerParams(
            collective_id=0, has_side_effects=True, vmem_limit_bytes=58 * 1024 * 1024
        ),
    )(
        node_feats,
        send_rows,
        neighbors,
        neighbor_weight,
        gcn_weight,
        user_dense,
        cand_owner.reshape(REQS, CAND),
        cand_row,
        mlp_weight,
        out_weight.reshape(1, -1),
        logit_grad.reshape(REQS, 1),
    )
    return (embeddings, embed_grad, clicks[:, 0], mean.astype(F32))


def solution(mesh):
    return jax.shard_map(
        on_device,
        mesh=mesh,
        in_specs=(
            P(("shard", "rep"), None),
            P(("shard", "rep"), None, None),
            P(("shard", "rep"), None),
            P(("shard", "rep"), None),
            P(),
            P(("shard", "rep"), None),
            P(("shard", "rep"), None, None),
            P(("shard", "rep"), None),
            P(),
            P(),
            P(("shard", "rep")),
        ),
        out_specs=(P(("shard", "rep"), None), P(("shard", "rep"), None), P(("shard", "rep")), P()),
        check_vma=False,
    )
```

```python
import math

import jax
import jax.numpy as jnp
from jax import lax
from jax.experimental import pallas as pl
from jax.experimental.pallas import tpu as pltpu
from jax.sharding import PartitionSpec as P

MESH = pl.DeviceIdType.MESH
F32, BF16, I32 = jnp.float32, jnp.bfloat16, jnp.int32
N_X, N_Y, N_Z, GROUP = 4, 8, 12, 16
NODES, WIDTH, DEG, BND = 256, 512, 16, 32
REQS, CAND, PAD, CAP = 8, 50, 64, 56
SLOTS = REQS * PAD
LINES = SLOTS + NODES
PAIRS = CAND * (CAND + 1) // 2
CHUNKS = 2
ROOT = 1.0 / math.sqrt(WIDTH)


def mm(a, b):
    return lax.dot_general(a, b, (((1,), (0,)), ((), ())), preferred_element_type=F32)


def nt(a, b):
    return lax.dot_general(a, b, (((1,), (1,)), ((), ())), preferred_element_type=F32)


def tn(a, b):
    return lax.dot_general(a, b, (((0,), (0,)), ((), ())), preferred_element_type=F32)


def iota(shape, axis):
    return lax.broadcasted_iota(I32, shape, axis)


def mark(condition):
    return jnp.where(condition, 1.0, 0.0).astype(BF16)


def rows_at(start, count, unit):
    return pl.ds(pl.multiple_of(start, unit), count)


def wide(column, times):
    return jnp.concatenate([column] * times, axis=1)


def kernel(
    feats,
    send_rows,
    neighbors,
    weights,
    gcn_hbm,
    user,
    owners,
    wanted,
    mlp_hbm,
    out_weight,
    logit_grad,
    emb_out,
    grad_out,
    click_out,
    mean_out,
    lists,
    meta,
    table,
    place,
    msg_out,
    msg_in,
    choose,
    drawn,
    held_by,
    flat,
    bound,
    wsum,
    acc,
    joined,
    unit,
    inv,
    stack,
    grams,
    lower,
    pair_grad,
    cand_grad,
    pre_grad,
    term,
    outbox,
    inbox,
    spread,
    mlp,
    gcn,
    send0,
    recv0,
    half,
    send1,
    recv1,
    tiled,
    send2,
    recv2,
    slots3,
    fin4,
    fin5,
    fin6,
    w_sem,
    meta_s,
    meta_r,
    metac_s,
    metac_r,
    feat_s,
    feat_r,
    featc_s,
    featc_r,
    msg_s,
    msg_r,
    box_s,
    box_r,
    red_s,
    red_r,
):
    shard, rep = lax.axis_index("shard"), lax.axis_index("rep")
    y, core = lax.div(shard, 2), lax.rem(shard, 2)
    z, x = lax.div(rep, N_X), lax.rem(rep, N_X)
    me = shard

    def at_shard(k):
        return {"shard": lax.rem(shard + k, GROUP)}

    def at_x(k):
        return {"rep": z * N_X + lax.rem(x + k, N_X)}

    def at_y(k):
        return {"shard": lax.rem(y + k, N_Y) * 2 + core}

    def at_z(k):
        return {"rep": lax.rem(z + k, N_Z) * N_X + x}

    other_core = {"shard": y * 2 + 1 - core}
    right, left = at_y(1), at_y(N_Y - 1)

    peers = [at_shard(k) for k in range(1, GROUP)]
    peers += [at_x(k) for k in range(1, N_X)] + [at_z(k) for k in range(1, N_Z)]
    barrier = pltpu.get_barrier_semaphore()
    for peer in peers:
        pl.semaphore_signal(barrier, inc=1, device_id=peer, device_id_type=MESH)

    local = [
        pltpu.make_async_copy(gcn_hbm, gcn, w_sem.at[0]),
        pltpu.make_async_copy(mlp_hbm, mlp, w_sem.at[1]),
    ]
    for copy in local:
        copy.start()

    sent = []

    def send(src, dst, s_sem, r_sem, peer):
        copy = pltpu.make_async_remote_copy(
            src_ref=src,
            dst_ref=dst,
            send_sem=s_sem,
            recv_sem=r_sem,
            device_id=peer,
            device_id_type=MESH,
        )
        copy.start()
        sent.append(copy)
        return copy

    ids = neighbors[...]
    lists[0:DEG, :] = lax.shift_right_logical(ids, 5).astype(F32)
    lists[DEG : 2 * DEG, :] = jnp.bitwise_and(ids, BND - 1).astype(F32)
    lists[2 * DEG : 3 * DEG, :] = weights[...]
    lists[3 * DEG :, :] = jnp.zeros((DEG, NODES), F32)
    sr = send_rows[0].astype(F32).astype(BF16)
    sr = mm(sr, mark(jnp.bitwise_and(iota((BND, NODES), 1), BND - 1) == iota((BND, NODES), 0)))
    for part in range(2):
        owner_of = lax.shift_right_logical(iota((GROUP, NODES), 1), 5) + part * 8
        line = jnp.sum(jnp.where(iota((GROUP, NODES), 0) == owner_of, sr, 0.0), axis=0, keepdims=True)
        lists[3 * DEG + part : 3 * DEG + part + 1, :] = line
    meta[me] = lists[...].astype(BF16)
    table[y, rows_at(core * NODES, NODES, NODES), :] = feats[...]

    pl.semaphore_wait(barrier, len(peers))

    def chip(d):
        return lax.rem(y + d + N_Y, N_Y)

    meta_got, metac_got, feat_got, featc_got = {}, {}, {}, {}

    def meta_ring(way, hop):
        block = chip(-hop if way == 0 else hop) * 2 + core
        ref = meta.at[block]
        number = way * 4 + hop
        meta_got[way, hop] = send(
            ref, ref, meta_s.at[number], meta_r.at[number], right if way == 0 else left
        )

    def meta_core(d, number):
        ref = meta.at[chip(d) * 2 + core]
        metac_got[d] = send(ref, ref, metac_s.at[number], metac_r.at[number], other_core)

    def feat_ref(d, part):
        return table.at[chip(d), rows_at(core * NODES + part * 128, 128, 128)]

    def feat_ring(way, hop, part):
        ref = feat_ref(-hop if way == 0 else hop, part)
        number = (way * 4 + hop) * 2 + part
        feat_got[way, hop, part] = send(
            ref, ref, feat_s.at[number], feat_r.at[number], right if way == 0 else left
        )

    core_order = (0, -1, 1, -2, 2, -3, 3, 4)

    def feat_core(d, part):
        number = core_order.index(d) * 2 + part
        ref = feat_ref(d, part)
        featc_got[d, part] = send(ref, ref, featc_s.at[number], featc_r.at[number], other_core)

    def meta_step(hop):
        meta_got[0, hop].wait_recv()
        if hop < 3:
            meta_ring(0, hop + 1)
            meta_got[1, hop].wait_recv()
            if hop < 2:
                meta_ring(1, hop + 1)
            meta_core(-1 - hop, 1 + 2 * hop)
            meta_core(1 + hop, 2 + 2 * hop)
        else:
            meta_core(4, 7)

    def feat_step(hop, part):
        if hop < 3:
            feat_got[0, hop, part].wait_recv()
            if hop < 2 or part == 0:
                feat_ring(0, hop + 1, part)
            feat_got[1, hop, part].wait_recv()
            if hop < 2 or part == 1:
                feat_ring(1, hop + 1, part)
            feat_core(-1 - hop, part)
            feat_core(1 + hop, part)
        else:
            feat_got[part, hop, part].wait_recv()
            feat_core(4, part)

    meta_ring(0, 0)
    meta_ring(1, 0)
    meta_core(0, 0)
    for part in range(2):
        feat_ring(0, 0, part)
        feat_ring(1, 0, part)
    for part in range(2):
        feat_core(0, part)

    request = lax.shift_right_logical(iota((SLOTS, REQS), 0), 6)
    of_request = mark(request == iota((SLOTS, REQS), 1))
    within = jnp.bitwise_and(iota((SLOTS, CAND), 0), PAD - 1)
    hit = iota((SLOTS, CAND), 1) == within - 1
    spot = jnp.bitwise_and(iota((SLOTS, 128), 0), PAD - 1)
    valid = (spot >= 1) & (spot <= CAND)

    def column(values):
        spread_out = mm(of_request, values.astype(F32).astype(BF16))
        return mm(jnp.where(hit, spread_out, 0.0).astype(BF16), jnp.ones((CAND, 128), BF16))

    owner_col = jnp.where(valid, column(owners[...]), -1.0)
    row_col = jnp.where(valid, column(wanted[...]), 0.0)
    owner16, row16 = owner_col.astype(BF16), row_col.astype(BF16)

    ones16 = jnp.ones((SLOTS, 128), BF16)
    zero16 = jnp.zeros((SLOTS, 128), BF16)
    lane_lo = iota((SLOTS, 128), 1).astype(F32).astype(BF16)
    lane_hi = (iota((SLOTS, 128), 1) + 128).astype(F32).astype(BF16)

    def choose_self(p, carry):
        here = jnp.where(owner16 == p.astype(F32).astype(BF16), row16, -ones16)
        choose[p, 0:SLOTS, 0:128] = jnp.where(here == lane_lo, ones16, zero16)
        choose[p, 0:SLOTS, 128:256] = jnp.where(here == lane_hi, ones16, zero16)
        return carry

    lax.fori_loop(0, GROUP, choose_self, 0)

    meta_step(0)

    lanes = iota((SLOTS, 128), 1).astype(F32)
    hits = mark(owner_col == lanes)
    below = mark(iota((SLOTS, SLOTS), 0) >= iota((SLOTS, SLOTS), 1))
    counts = mm(below, hits)
    rank = mm((jnp.where(owner_col == lanes, counts, 0.0)).astype(BF16), jnp.ones((128, 128), BF16))
    rank_lane = jnp.broadcast_to((rank - 1.0).T[0:1, :], (64, SLOTS)).astype(BF16)
    owner_lane = jnp.broadcast_to(owner_col.T[0:1, :], (64, SLOTS)).astype(BF16)
    row_lane = row_col.T[0:16, :].astype(BF16)
    feat_step(0, 0)
    meta_step(1)

    def place_owner(owner, carry):
        nobody = jnp.full((64, SLOTS), -1.0, BF16)
        at = jnp.where(owner_lane == owner.astype(F32).astype(BF16), rank_lane, nobody)
        goal = iota((64, SLOTS), 0).astype(F32).astype(BF16)
        place[rows_at(owner * 64, 64, 64), :] = jnp.where(at == goal, nobody * nobody, nobody * 0)
        return carry

    lax.fori_loop(0, GROUP, place_owner, 0)
    feat_step(0, 1)
    meta_step(2)
    notes = nt(row_lane, place[...]).astype(BF16)
    for two in range(GROUP // 2):
        msg_out[two] = notes[:, two * 128 : two * 128 + 128]
    msg_in[me] = msg_out[y]
    feat_step(1, 0)
    meta_step(3)
    for d in core_order:
        metac_got[d].wait_recv()

    def list_of(p, total):
        return total + nt(choose[p, 0:SLOTS, :], meta[p, 0 : 3 * DEG, :])

    got = lax.fori_loop(0, GROUP, list_of, jnp.zeros((SLOTS, 3 * DEG), F32))
    own = nt(mark(iota((NODES, NODES), 0) == iota((NODES, NODES), 1)), meta[me, 0 : 3 * DEG, :])
    drawn[:, 3 * DEG :] = jnp.zeros((LINES, 128 - 3 * DEG), F32)
    drawn[:, 0 : 3 * DEG] = jnp.concatenate([got, own], axis=0)
    held_by[0:SLOTS, :] = owner_col
    held_by[SLOTS:, :] = jnp.zeros((NODES, 128), F32) + me.astype(F32)
    got = drawn[:, 0 : 3 * DEG].astype(BF16)
    wsum[...] = mm(got, mark(iota((3 * DEG, 128), 0) >= 2 * DEG))
    batches = LINES // 16
    group_of = lax.shift_right_logical(iota((batches, 128), 1), 4)
    laid = [[jnp.zeros((batches, 128), F32) for _ in range(2)] for _ in range(4)]
    for c in range(16):
        here = group_of == c % 8
        every = pl.ds(c, batches, stride=16)
        lines = drawn[every, :]
        for field in range(3):
            turn = (c - field) * DEG % 128
            line = pltpu.roll(lines, turn, 1) if turn else lines
            laid[field][c // 8] = jnp.where(here, line, laid[field][c // 8])
        laid[3][c // 8] = jnp.where(here, held_by[every, :], laid[3][c // 8])
    part_of, rest, share, keeper = [jnp.concatenate(halves, axis=1) for halves in laid]
    inside = part_of < NODES // BND
    source = jnp.where(inside, keeper, part_of - NODES // BND)
    which = keeper * BND + rest
    member_at = lax.shift_right_logical(iota((batches, 256), 1), 4).astype(F32)
    for number, values in enumerate((
        source * 16 + member_at,
        jnp.where(inside, part_of * BND + rest, -1.0),
        share,
        jnp.where(inside | (which >= 256), -1.0, which),
        jnp.where(inside | (which < 256), -1.0, which - 256),
        source,
    )):
        flat[:, number * 256 : number * 256 + 256] = values
    all_bounds = meta[:, 3 * DEG : 4 * DEG, :].reshape(GROUP * 16, NODES)
    for part in range(2):
        pick = mark(iota((GROUP, GROUP * 16), 1) == iota((GROUP, GROUP * 16), 0) * 16 + part)
        bound[part] = mm(pick, all_bounds).astype(BF16)
    feat_step(1, 1)

    def build_one(batch):
        one, nothing = jnp.ones((16, 256), BF16), jnp.zeros((16, 256), BF16)

        def line(field):
            return flat[pl.ds(batch, 1), field * 256 : field * 256 + 256]

        def tall(values):
            return jnp.broadcast_to(values, (16, 256)).astype(BF16)

        def chart(values, entry):
            strips = []
            for i in range(16):
                goal = (iota((16, 256), 0) + i * 16).astype(F32).astype(BF16)
                strips.append(jnp.where(values == goal, entry, nothing))
            return jnp.concatenate(strips, axis=0)

        far = mm(bound[0], chart(tall(line(3)), one)) + mm(bound[1], chart(tall(line(4)), one))
        far = jnp.where(iota((GROUP, 256), 0).astype(F32) == line(5), far, 0.0)
        near = line(1)
        low = jnp.where(near < 0, jnp.sum(far, axis=0, keepdims=True), near)
        mixed = nt(chart(tall(line(0)), tall(line(2))), chart(tall(low), one)).astype(BF16)
        choose[:, rows_at(SLOTS + batch * 16, 16, 16), :] = mixed.reshape(GROUP, 16, 256)

    def build(pair, carry):
        build_one(pair * 2)
        build_one(pair * 2 + 1)
        return carry

    def absorb(chips, first=False):
        blocks = [chip(d) for d in chips]
        for d in chips:
            for part in range(2):
                featc_got[d, part].wait_recv()

        def rows_of(tile, carry):
            rows = rows_at(tile * 256, 256, 256)
            product = None if first else acc[rows, :]
            for block in blocks:
                for i in range(2):
                    more = mm(choose[block * 2 + i, rows, :], table[block, i * NODES : (i + 1) * NODES, :])
                    product = more if product is None else product + more
            acc[rows, :] = product
            return carry

        lax.fori_loop(0, 2 * SLOTS // 256, rows_of, 0)

    lax.fori_loop(0, 8, build, 0)
    feat_step(2, 0)
    lax.fori_loop(8, SLOTS // 32, build, 0)
    absorb((0,), True)
    feat_step(2, 1)
    absorb((-1, 1))
    absorb((-2, 2))
    feat_step(3, 0)
    feat_step(3, 1)
    absorb((-3, 3))
    absorb((4,))
    msg_got = []
    for k in range(1, GROUP):
        to = lax.div(lax.rem(me + k, GROUP), 2)
        msg_got.append(send(msg_out.at[to], msg_in.at[me], msg_s.at[k - 1], msg_r.at[k - 1], at_shard(k)))

    local[0].wait()

    def embed(tile, carry):
        rows = rows_at(tile * 256, 256, 256)
        sums = wsum[rows, :]
        scale = 1.0 / jnp.where(sums > 0, sums, 1.0)
        itself = acc[rows, :].astype(BF16)
        around = (acc[rows_at(SLOTS + tile * 256, 256, 256), :] * wide(scale, 4)).astype(BF16)
        joined[rows, 0:WIDTH] = itself
        joined[rows, WIDTH:] = around
        projected = mm(itself, gcn[0:WIDTH, :]) + mm(around, gcn[WIDTH:, :])
        root = lax.rsqrt(jnp.mean(projected * projected, axis=-1, keepdims=True) + 1e-06)
        ready = projected * root
        unit[rows, :] = ready
        inv[rows, :] = jnp.broadcast_to(root, (256, 128))
        line = iota((256, REQS), 0) + tile * 256
        users = mm(mark(lax.shift_right_logical(line, 6) == iota((256, REQS), 1)), user[...])
        is_user = jnp.bitwise_and(iota((256, WIDTH), 0), PAD - 1) == 0
        stack[rows, :] = jnp.where(is_user, users, ready).astype(BF16)
        return carry

    lax.fori_loop(0, SLOTS // 256, embed, 0)
    stack[SLOTS : SLOTS + PAD, :] = jnp.zeros((PAD, WIDTH), BF16)

    def gram(q, carry):
        grams[q] = nt(stack[rows_at(q * PAD, PAD, PAD), :], stack[rows_at(q * PAD, 2 * PAD, PAD), :]) * ROOT
        return carry

    lax.fori_loop(0, REQS, gram, 0)

    lane8 = iota((REQS, 128), 1)
    strips = [jnp.zeros((REQS, 128), F32) for _ in range(PAIRS // 128 + 2)]
    for i in range(1, CAND + 1):
        strip, shift = divmod(i * (i - 1) // 2, 128)
        line = jnp.where(lane8 < i, grams[:, i, :], 0.0)
        if shift:
            line = pltpu.roll(line, shift, 1)
        if shift + i > 128:
            strips[strip] = strips[strip] + jnp.where(lane8 >= shift, line, 0.0)
            strips[strip + 1] = strips[strip + 1] + jnp.where(lane8 < shift, line, 0.0)
        else:
            strips[strip] = strips[strip] + line
    whole = PAIRS // 128 * 128
    pairs = jnp.concatenate(strips[: PAIRS // 128], axis=1).astype(BF16)
    tail = strips[PAIRS // 128][:, 0 : PAIRS - whole].astype(BF16)

    local[1].wait()
    split = WIDTH + whole
    pre = mm(user[...], mlp[0:WIDTH, :]) + mm(pairs, mlp[WIDTH:split, :])
    pre = pre + mm(tail, mlp[split : WIDTH + PAIRS, :])
    bend = math.sqrt(2.0 / math.pi)
    curve = jnp.tanh(bend * (pre + 0.044715 * (pre * pre * pre)))
    hidden = (pre * (0.5 * (1.0 + curve))).astype(BF16)
    out_w = out_weight[...].astype(F32).reshape(1, -1)
    click_out[...] = nt(jnp.broadcast_to(out_w, (REQS, out_w.shape[1])).astype(BF16), hidden)[0]
    given_logit = jnp.zeros((REQS, 1), F32)
    for q in range(REQS):
        given_logit = jnp.where(iota((REQS, 1), 0) == q, logit_grad[q], given_logit)
    slope = 0.5 * (1.0 + curve) + 0.5 * pre * (1.0 - curve * curve) * bend * (1.0 + 3 * 0.044715 * pre * pre)
    hidden_grad = (given_logit * out_w * slope).astype(BF16)
    pair_grad[:, whole:] = jnp.zeros((REQS, 128), F32)
    pair_grad[:, 0:whole] = nt(hidden_grad, mlp[WIDTH:split, :])
    pair_grad[:, whole:PAIRS] = nt(hidden_grad, mlp[split : WIDTH + PAIRS, :])

    lower[...] = jnp.zeros((REQS, PAD, 128), F32)
    for i in range(1, CAND + 1):
        strip, shift = divmod(i * (i - 1) // 2, 128)
        line = pair_grad[:, strip * 128 : strip * 128 + 128]
        if shift:
            line = pltpu.roll(line, 128 - shift, 1)
        if shift + i > 128:
            more = pltpu.roll(pair_grad[:, strip * 128 + 128 : strip * 128 + 256], 128 - shift, 1)
            line = jnp.where(lane8 < 128 - shift, line, more)
        lower[:, i, :] = jnp.where(lane8 < i, line, 0.0)

    def back(q, carry):
        under = lower[q]
        both = (under[:, 0:PAD] + under.T[0:PAD, :]).astype(BF16)
        rows = rows_at(q * PAD, PAD, PAD)
        grad = mm(both, stack[rows, :]) * ROOT
        row = iota((PAD, WIDTH), 0)
        grad = jnp.where((row >= 1) & (row <= CAND), grad, 0.0).astype(BF16)
        cand_grad[rows, :] = grad
        ready, given = unit[rows, :], grad.astype(F32)
        along = jnp.mean(ready * given, axis=-1, keepdims=True)
        pre_grad[rows, :] = (wide(inv[rows, :], 4) * (given - ready * along)).astype(BF16)
        return carry

    lax.fori_loop(0, REQS, back, 0)

    def fill(four, carry):
        picked = mm(place[rows_at(four * 256, 256, 256), :], cand_grad[...])
        for j in range(4):
            one = picked[j * 64 : j * 64 + CAP]
            both = jnp.concatenate([one[:, 0 : WIDTH // 2], one[:, WIDTH // 2 :]], axis=0)
            outbox[four * 4 + j] = both.astype(BF16)
        return carry

    lax.fori_loop(0, 4, fill, 0)
    my_box = inbox.at[rows_at(me * 2 * CAP, 2 * CAP, 16)]
    box_got = []

    def send_boxes(steps_away):
        for k in steps_away:
            to = lax.rem(me + k, GROUP)
            box_got.append(send(outbox.at[to], my_box, box_s.at[k - 1], box_r.at[k - 1], at_shard(k)))

    send_boxes((8, 7, 9, 6, 10, 1, 15, 2, 14, 3, 13))
    kept = pltpu.make_async_copy(outbox.at[me], my_box, w_sem.at[2])
    kept.start()

    def weight_term(tile, carry):
        cols = rows_at(tile * 256, 256, 256)
        term[cols, :] = tn(joined[:, cols], pre_grad[...])
        return carry

    lax.fori_loop(0, 4, weight_term, 0)

    rows, width = term.shape
    chunk = width // CHUNKS
    in_flight = {}

    def pass_on(c, number, src, dst, peer):
        in_flight[c, number] = send(src, dst, red_s.at[c, number], red_r.at[c, number], peer)

    def arrive(c, numbers):
        for number in numbers:
            in_flight[c, number].wait_recv()

    def step0(c):
        theirs = pl.multiple_of((1 - core) * (rows // 2), rows // 2)
        send0[c] = term[pl.ds(theirs, rows // 2), c * chunk : (c + 1) * chunk].astype(BF16)
        pass_on(c, 0, send0.at[c], recv0.at[c], other_core)

    def step1(c):
        arrive(c, [0])
        mine = pl.multiple_of(core * (rows // 2), rows // 2)
        total = term[pl.ds(mine, rows // 2), c * chunk : (c + 1) * chunk] + recv0[c].astype(F32)
        half[c] = total.reshape(N_X, rows // 8, chunk)
        send1[c] = total.astype(BF16).reshape(N_X, rows // 8, chunk)
        for k in range(1, N_X):
            to = lax.rem(x + k, N_X)
            pass_on(c, k, send1.at[c, to], recv1.at[c, k - 1], at_x(k))

    def step2(c):
        arrive(c, range(1, 4))
        total = half[c, x]
        for k in range(N_X - 1):
            total = total + recv1[c, k].astype(F32)
        for j in range(chunk // 128):
            tiles = total[:, j * 128 : j * 128 + 128].reshape(8, 16, 128)
            tiled[c, j * 8 : j * 8 + 8] = tiles
            send2[c, j * 8 : j * 8 + 8] = tiles.astype(BF16)
        tiled[c, 16:24] = jnp.zeros((8, 16, 128), F32)
        send2[c, 16:24] = jnp.zeros((8, 16, 128), BF16)
        for k in range(1, N_Z):
            to = lax.rem(z + k, N_Z)
            pass_on(c, 3 + k, send2.at[c, pl.ds(to * 2, 2)], recv2.at[c, k - 1], at_z(k))

    def step3(c):
        arrive(c, range(4, 15))
        total = tiled[c, pl.ds(z * 2, 2)]
        for k in range(N_Z - 1):
            total = total + recv2[c, k].astype(F32)
        slots3[c, y] = total.astype(BF16)
        for k in range(1, N_Y):
            pass_on(c, 14 + k, slots3.at[c, y], slots3.at[c, y], at_y(k))

    def step4(c):
        arrive(c, range(15, 22))
        total = slots3[c, 0].astype(F32)
        for k in range(1, N_Y):
            total = total + slots3[c, k].astype(F32)
        fin4[c, z] = (total * (1.0 / (GROUP * N_X * N_Z))).astype(BF16)
        for k in range(1, N_Z):
            pass_on(c, 21 + k, fin4.at[c, z], fin4.at[c, z], at_z(k))

    def step5(c):
        arrive(c, range(22, 33))
        fin5[c, x] = fin4[c].reshape(24, 16, 128)[0:16]
        for k in range(1, N_X):
            pass_on(c, 32 + k, fin5.at[c, x], fin5.at[c, x], at_x(k))

    def step6(c):
        arrive(c, range(33, 36))
        fin6[c, core] = fin5[c]
        pass_on(c, 36, fin6.at[c, core], fin6.at[c, core], other_core)

    def step7(c):
        arrive(c, [36])
        for j in range(chunk // 128):
            done = fin6[c, :, :, j * 8 : j * 8 + 8].reshape(rows, 128)
            mean_out[:, c * chunk + j * 128 : c * chunk + j * 128 + 128] = done

    steps = (step0, step1, step2, step3, step4, step5, step6, step7)
    waves = [
        [(wave - c, c) for c in range(CHUNKS) if 0 <= wave - c < len(steps)]
        for wave in range(len(steps) + CHUNKS - 1)
    ]

    def run(wave):
        for step, c in waves[wave]:
            steps[step](c)

    run(0)
    run(1)
    lax.fori_loop(SLOTS // 32, LINES // 32, build, 0)
    run(2)

    def own_part(p, total):
        block = table[lax.div(p, 2), rows_at(lax.rem(p, 2) * NODES, NODES, NODES), :]
        return total + mm(choose[p, 2 * SLOTS :, :], block)

    shares = lax.fori_loop(0, GROUP, own_part, jnp.zeros((NODES, WIDTH), F32))
    around = (shares * wide(1.0 / wsum[SLOTS:, :], 4)).astype(BF16)
    projected = mm(feats[...], gcn[0:WIDTH, :]) + mm(around, gcn[WIDTH:, :])
    root = lax.rsqrt(jnp.mean(projected * projected, axis=-1, keepdims=True) + 1e-06)
    emb_out[...] = (projected * root).astype(BF16)
    run(3)

    for copy in msg_got:
        copy.wait_recv()
    box_rows = GROUP * 2 * CAP
    lane16 = iota((16, 128), 1)
    marks = [jnp.zeros((16, 128), F32) for _ in range(box_rows // 128 + 1)]
    for p in range(GROUP):
        strip, shift = divmod(p * 2 * CAP, 128)
        line = msg_in[p].astype(F32)
        line = jnp.where(core == 1, pltpu.roll(line, 64, 1), line)
        line = jnp.where(lane16 < CAP, line, 0.0)
        line = line + pltpu.roll(line, CAP, 1)
        if shift:
            line = pltpu.roll(line, shift, 1)
        if shift + 2 * CAP > 128:
            marks[strip] = marks[strip] + jnp.where(lane16 >= shift, line, 0.0)
            marks[strip + 1] = marks[strip + 1] + jnp.where(lane16 < shift, line, 0.0)
        else:
            marks[strip] = marks[strip] + line
    run(4)
    send_boxes((4, 12, 5, 11))
    for strip in range(box_rows // 128):
        line = lax.rem(iota((1, 128), 1) + strip * 128, 2 * CAP)
        goal = marks[strip][0:1, :]
        cols = slice(strip * 128, strip * 128 + 128)
        here = iota((NODES, 128), 0).astype(F32)
        spread[0:NODES, cols] = mark(here == jnp.where(line < CAP, goal, -1.0))
        spread[NODES:, cols] = mark(here == jnp.where(line < CAP, -1.0, goal))
    for wave in range(5, len(waves)):
        run(wave)

    for copy in box_got:
        copy.wait_recv()
    kept.wait()
    for part in range(2):
        cols = slice(part * NODES, part * NODES + NODES)
        grad_out[:, cols] = mm(spread[cols, :], inbox[...])
    for copy in sent:
        copy.wait_send()


def on_device(
    node_feats,
    send_rows,
    neighbors,
    neighbor_weight,
    gcn_weight,
    user_dense,
    cand_owner,
    cand_row,
    mlp_weight,
    out_weight,
    logit_grad,
):
    rows, width = gcn_weight.shape
    chunk = width // CHUNKS
    eighth = rows // 8
    vmem = pl.BlockSpec(memory_space=pltpu.VMEM)
    hbm = pl.BlockSpec(memory_space=pl.ANY)
    smem = pl.BlockSpec(memory_space=pltpu.SMEM)
    dma = pltpu.SemaphoreType.DMA
    embeddings, embed_grad, clicks, mean = pl.pallas_call(
        kernel,
        out_shape=(
            jax.ShapeDtypeStruct((NODES, WIDTH), BF16),
            jax.ShapeDtypeStruct((NODES, WIDTH), F32),
            jax.ShapeDtypeStruct((REQS,), F32),
            jax.ShapeDtypeStruct((rows, width), BF16),
        ),
        in_specs=[vmem, vmem, vmem, vmem, hbm, vmem, vmem, vmem, hbm, vmem, smem],
        out_specs=(vmem, vmem, vmem, vmem),
        scratch_shapes=[
            pltpu.VMEM((4 * DEG, NODES), F32),
            pltpu.VMEM((GROUP, 4 * DEG, NODES), BF16),
            pltpu.VMEM((N_Y, 2 * NODES, WIDTH), BF16),
            pltpu.VMEM((GROUP * 64, SLOTS), BF16),
            pltpu.VMEM((GROUP // 2, 16, 128), BF16),
            pltpu.VMEM((GROUP, 16, 128), BF16),
            pltpu.VMEM((GROUP, SLOTS + LINES, NODES), BF16),
            pltpu.VMEM((LINES, 128), F32),
            pltpu.VMEM((LINES, 128), F32),
            pltpu.VMEM((LINES // 16, 6 * 256), F32),
            pltpu.VMEM((2, GROUP, NODES), BF16),
            pltpu.VMEM((LINES, 128), F32),
            pltpu.VMEM((2 * SLOTS, WIDTH), F32),
            pltpu.VMEM((SLOTS, 2 * WIDTH), BF16),
            pltpu.VMEM((SLOTS, WIDTH), F32),
            pltpu.VMEM((SLOTS, 128), F32),
            pltpu.VMEM((SLOTS + PAD, WIDTH), BF16),
            pltpu.VMEM((REQS, PAD, 128), F32),
            pltpu.VMEM((REQS, PAD, 128), F32),
            pltpu.VMEM((REQS, PAIRS // 128 * 128 + 128), F32),
            pltpu.VMEM((SLOTS, WIDTH), BF16),
            pltpu.VMEM((SLOTS, WIDTH), BF16),
            pltpu.VMEM((rows, width), F32),
            pltpu.VMEM((GROUP, 2 * CAP, WIDTH // 2), BF16),
            pltpu.VMEM((GROUP * 2 * CAP, WIDTH // 2), BF16),
            pltpu.VMEM((2 * NODES, GROUP * 2 * CAP), BF16),
            pltpu.VMEM(mlp_weight.shape, BF16),
            pltpu.VMEM((rows, width), BF16),
            pltpu.VMEM((CHUNKS, rows // 2, chunk), BF16),
            pltpu.VMEM((CHUNKS, rows // 2, chunk), BF16),
            pltpu.VMEM((CHUNKS, N_X, eighth, chunk), F32),
            pltpu.VMEM((CHUNKS, N_X, eighth, chunk), BF16),
            pltpu.VMEM((CHUNKS, N_X - 1, eighth, chunk), BF16),
            pltpu.VMEM((CHUNKS, 24, 16, 128), F32),
            pltpu.VMEM((CHUNKS, 24, 16, 128), BF16),
            pltpu.VMEM((CHUNKS, N_Z - 1, 2, 16, 128), BF16),
            pltpu.VMEM((CHUNKS, N_Y, 2, 16, 128), BF16),
            pltpu.VMEM((CHUNKS, N_Z, 2, 16, 128), BF16),
            pltpu.VMEM((CHUNKS, N_X, 16, 16, 128), BF16),
            pltpu.VMEM((CHUNKS, 2, N_X, 16, 16, 128), BF16),
            dma((3,)),
            dma((8,)),
            dma((8,)),
            dma((8,)),
            dma((8,)),
            dma((16,)),
            dma((16,)),
            dma((16,)),
            dma((16,)),
            dma((GROUP - 1,)),
            dma((GROUP - 1,)),
            dma((GROUP - 1,)),
            dma((GROUP - 1,)),
            dma((CHUNKS, 37)),
            dma((CHUNKS, 37)),
        ],
        compiler_params=pltpu.CompilerParams(
            collective_id=0, has_side_effects=True, vmem_limit_bytes=58 * 1024 * 1024
        ),
    )(
        node_feats,
        send_rows,
        neighbors.T,
        neighbor_weight.T,
        gcn_weight,
        user_dense,
        cand_owner.reshape(REQS, CAND),
        cand_row,
        mlp_weight,
        out_weight,
        logit_grad,
    )
    return (embeddings, embed_grad, clicks, mean.astype(F32))


def solution(mesh):
    return jax.shard_map(
        on_device,
        mesh=mesh,
        in_specs=(
            P(("shard", "rep"), None),
            P(("shard", "rep"), None, None),
            P(("shard", "rep"), None),
            P(("shard", "rep"), None),
            P(),
            P(("shard", "rep"), None),
            P(("shard", "rep"), None, None),
            P(("shard", "rep"), None),
            P(),
            P(),
            P(("shard", "rep")),
        ),
        out_specs=(P(("shard", "rep"), None), P(("shard", "rep"), None), P(("shard", "rep")), P()),
        check_vma=False,
    )
```

```python
import math

import jax
import jax.numpy as jnp
from jax import lax
from jax.experimental import pallas as pl
from jax.experimental.pallas import tpu as pltpu
from jax.sharding import PartitionSpec as P

MESH = pl.DeviceIdType.MESH
F32, BF16, I32 = jnp.float32, jnp.bfloat16, jnp.int32
N_X, N_Y, N_Z, GROUP = 4, 8, 12, 16
NODES, WIDTH, DEG, BND = 256, 512, 16, 32
REQS, CAND, PAD, CAP = 8, 50, 64, 56
SLOTS = REQS * PAD
LINES = SLOTS + NODES
PAIRS = CAND * (CAND + 1) // 2
CHUNKS = 2
ROOT = 1.0 / math.sqrt(WIDTH)


def mm(a, b):
    return lax.dot_general(a, b, (((1,), (0,)), ((), ())), preferred_element_type=F32)


def nt(a, b):
    return lax.dot_general(a, b, (((1,), (1,)), ((), ())), preferred_element_type=F32)


def tn(a, b):
    return lax.dot_general(a, b, (((0,), (0,)), ((), ())), preferred_element_type=F32)


def iota(shape, axis):
    return lax.broadcasted_iota(I32, shape, axis)


def mark(condition):
    return jnp.where(condition, 1.0, 0.0).astype(BF16)


def rows_at(start, count, unit):
    return pl.ds(pl.multiple_of(start, unit), count)


def wide(column, times):
    return jnp.concatenate([column] * times, axis=1)


def kernel(
    feats,
    send_rows,
    neighbors,
    weights,
    gcn_hbm,
    user,
    owners,
    wanted,
    mlp_hbm,
    out_weight,
    logit_grad,
    emb_out,
    grad_out,
    click_out,
    mean_out,
    lists,
    meta,
    table,
    place,
    msg_out,
    msg_in,
    choose,
    drawn,
    held_by,
    flat,
    bound,
    wsum,
    acc,
    joined,
    unit,
    inv,
    stack,
    grams,
    lower,
    pair_grad,
    cand_grad,
    pre_grad,
    term,
    outbox,
    inbox,
    spread,
    mlp,
    gcn,
    send0,
    recv0,
    half,
    send1,
    recv1,
    tiled,
    send2,
    recv2,
    slots3,
    fin4,
    fin5,
    fin6,
    w_sem,
    meta_s,
    meta_r,
    metac_s,
    metac_r,
    feat_s,
    feat_r,
    featc_s,
    featc_r,
    msg_s,
    msg_r,
    box_s,
    box_r,
    red_s,
    red_r,
):
    shard, rep = lax.axis_index("shard"), lax.axis_index("rep")
    y, core = lax.div(shard, 2), lax.rem(shard, 2)
    z, x = lax.div(rep, N_X), lax.rem(rep, N_X)
    me = shard

    def at_shard(k):
        return {"shard": lax.rem(shard + k, GROUP)}

    def at_x(k):
        return {"rep": z * N_X + lax.rem(x + k, N_X)}

    def at_y(k):
        return {"shard": lax.rem(y + k, N_Y) * 2 + core}

    def at_z(k):
        return {"rep": lax.rem(z + k, N_Z) * N_X + x}

    other_core = {"shard": y * 2 + 1 - core}
    right, left = at_y(1), at_y(N_Y - 1)

    peers = [at_shard(k) for k in range(1, GROUP)]
    peers += [at_x(k) for k in range(1, N_X)] + [at_z(k) for k in range(1, N_Z)]
    barrier = pltpu.get_barrier_semaphore()
    for peer in peers:
        pl.semaphore_signal(barrier, inc=1, device_id=peer, device_id_type=MESH)

    local = [
        pltpu.make_async_copy(gcn_hbm, gcn, w_sem.at[0]),
        pltpu.make_async_copy(mlp_hbm, mlp, w_sem.at[1]),
    ]
    for copy in local:
        copy.start()

    sent = []

    def send(src, dst, s_sem, r_sem, peer):
        copy = pltpu.make_async_remote_copy(
            src_ref=src,
            dst_ref=dst,
            send_sem=s_sem,
            recv_sem=r_sem,
            device_id=peer,
            device_id_type=MESH,
        )
        copy.start()
        sent.append(copy)
        return copy

    ids = neighbors[...]
    lists[0:DEG, :] = lax.shift_right_logical(ids, 5).astype(F32)
    lists[DEG : 2 * DEG, :] = jnp.bitwise_and(ids, BND - 1).astype(F32)
    lists[2 * DEG : 3 * DEG, :] = weights[...]
    lists[3 * DEG :, :] = jnp.zeros((DEG, NODES), F32)
    sr = send_rows[0].astype(F32).astype(BF16)
    sr = mm(sr, mark(jnp.bitwise_and(iota((BND, NODES), 1), BND - 1) == iota((BND, NODES), 0)))
    for part in range(2):
        owner_of = lax.shift_right_logical(iota((GROUP, NODES), 1), 5) + part * 8
        line = jnp.sum(jnp.where(iota((GROUP, NODES), 0) == owner_of, sr, 0.0), axis=0, keepdims=True)
        lists[3 * DEG + part : 3 * DEG + part + 1, :] = line
    meta[me] = lists[...].astype(BF16)
    table[y, rows_at(core * NODES, NODES, NODES), :] = feats[...]

    pl.semaphore_wait(barrier, len(peers))

    def chip(d):
        return lax.rem(y + d + N_Y, N_Y)

    meta_got, metac_got, feat_got, featc_got = {}, {}, {}, {}

    def meta_ring(way, hop):
        block = chip(-hop if way == 0 else hop) * 2 + core
        ref = meta.at[block]
        number = way * 4 + hop
        meta_got[way, hop] = send(
            ref, ref, meta_s.at[number], meta_r.at[number], right if way == 0 else left
        )

    def meta_core(d, number):
        ref = meta.at[chip(d) * 2 + core]
        metac_got[d] = send(ref, ref, metac_s.at[number], metac_r.at[number], other_core)

    def feat_ref(d, part):
        return table.at[chip(d), rows_at(core * NODES + part * 128, 128, 128)]

    def feat_ring(way, hop, part):
        ref = feat_ref(-hop if way == 0 else hop, part)
        number = (way * 4 + hop) * 2 + part
        feat_got[way, hop, part] = send(
            ref, ref, feat_s.at[number], feat_r.at[number], right if way == 0 else left
        )

    core_order = (0, -1, 1, -2, 2, -3, 3, 4)

    def feat_core(d, part):
        number = core_order.index(d) * 2 + part
        ref = feat_ref(d, part)
        featc_got[d, part] = send(ref, ref, featc_s.at[number], featc_r.at[number], other_core)

    def meta_step(hop):
        meta_got[0, hop].wait_recv()
        if hop < 3:
            meta_ring(0, hop + 1)
            meta_got[1, hop].wait_recv()
            if hop < 2:
                meta_ring(1, hop + 1)
            meta_core(-1 - hop, 1 + 2 * hop)
            meta_core(1 + hop, 2 + 2 * hop)
        else:
            meta_core(4, 7)

    def feat_step(hop, part):
        if hop < 3:
            feat_got[0, hop, part].wait_recv()
            if hop < 2 or part == 0:
                feat_ring(0, hop + 1, part)
            feat_got[1, hop, part].wait_recv()
            if hop < 2 or part == 1:
                feat_ring(1, hop + 1, part)
            feat_core(-1 - hop, part)
            feat_core(1 + hop, part)
        else:
            feat_got[part, hop, part].wait_recv()
            feat_core(4, part)

    meta_ring(0, 0)
    meta_ring(1, 0)
    meta_core(0, 0)
    for part in range(2):
        feat_ring(0, 0, part)
        feat_ring(1, 0, part)
    for part in range(2):
        feat_core(0, part)

    request = lax.shift_right_logical(iota((SLOTS, REQS), 0), 6)
    of_request = mark(request == iota((SLOTS, REQS), 1))
    within = jnp.bitwise_and(iota((SLOTS, CAND), 0), PAD - 1)
    hit = iota((SLOTS, CAND), 1) == within - 1
    spot = jnp.bitwise_and(iota((SLOTS, 128), 0), PAD - 1)
    valid = (spot >= 1) & (spot <= CAND)

    def column(values):
        spread_out = mm(of_request, values.astype(F32).astype(BF16))
        return mm(jnp.where(hit, spread_out, 0.0).astype(BF16), jnp.ones((CAND, 128), BF16))

    owner_col = jnp.where(valid, column(owners[...]), -1.0)
    row_col = jnp.where(valid, column(wanted[...]), 0.0)
    owner16, row16 = owner_col.astype(BF16), row_col.astype(BF16)

    ones16 = jnp.ones((SLOTS, 128), BF16)
    zero16 = jnp.zeros((SLOTS, 128), BF16)
    lane_lo = iota((SLOTS, 128), 1).astype(F32).astype(BF16)
    lane_hi = (iota((SLOTS, 128), 1) + 128).astype(F32).astype(BF16)

    def choose_self(p, carry):
        here = jnp.where(owner16 == p.astype(F32).astype(BF16), row16, -ones16)
        choose[p, 0:SLOTS, 0:128] = jnp.where(here == lane_lo, ones16, zero16)
        choose[p, 0:SLOTS, 128:256] = jnp.where(here == lane_hi, ones16, zero16)
        return carry

    lax.fori_loop(0, GROUP, choose_self, 0)

    meta_step(0)

    lanes = iota((SLOTS, 128), 1).astype(F32)
    hits = mark(owner_col == lanes)
    below = mark(iota((SLOTS, SLOTS), 0) >= iota((SLOTS, SLOTS), 1))
    counts = mm(below, hits)
    rank = mm((jnp.where(owner_col == lanes, counts, 0.0)).astype(BF16), jnp.ones((128, 128), BF16))
    rank_lane = jnp.broadcast_to((rank - 1.0).T[0:1, :], (64, SLOTS)).astype(BF16)
    owner_lane = jnp.broadcast_to(owner_col.T[0:1, :], (64, SLOTS)).astype(BF16)
    row_lane = row_col.T[0:16, :].astype(BF16)
    feat_step(0, 0)
    meta_step(1)

    def place_owner(owner, carry):
        nobody = jnp.full((64, SLOTS), -1.0, BF16)
        at = jnp.where(owner_lane == owner.astype(F32).astype(BF16), rank_lane, nobody)
        goal = iota((64, SLOTS), 0).astype(F32).astype(BF16)
        place[rows_at(owner * 64, 64, 64), :] = jnp.where(at == goal, nobody * nobody, nobody * 0)
        return carry

    lax.fori_loop(0, GROUP, place_owner, 0)
    feat_step(0, 1)
    meta_step(2)
    notes = nt(row_lane, place[...]).astype(BF16)
    for two in range(GROUP // 2):
        msg_out[two] = notes[:, two * 128 : two * 128 + 128]
    msg_in[me] = msg_out[y]
    feat_step(1, 0)
    meta_step(3)
    for d in core_order:
        metac_got[d].wait_recv()

    def list_of(four, total):
        for i in range(4):
            p = four * 4 + i
            total = total + nt(choose[p, 0:SLOTS, :], meta[p, 0 : 3 * DEG, :])
        return total

    got = lax.fori_loop(0, GROUP // 4, list_of, jnp.zeros((SLOTS, 3 * DEG), F32))
    own = nt(mark(iota((NODES, NODES), 0) == iota((NODES, NODES), 1)), meta[me, 0 : 3 * DEG, :])
    feat_step(1, 1)
    drawn[:, 3 * DEG :] = jnp.zeros((LINES, 128 - 3 * DEG), F32)
    drawn[:, 0 : 3 * DEG] = jnp.concatenate([got, own], axis=0)
    held_by[0:SLOTS, :] = owner_col
    held_by[SLOTS:, :] = jnp.zeros((NODES, 128), F32) + me.astype(F32)
    got = drawn[:, 0 : 3 * DEG].astype(BF16)
    wsum[...] = mm(got, mark(iota((3 * DEG, 128), 0) >= 2 * DEG))
    batches = LINES // 16
    group_of = lax.shift_right_logical(iota((batches, 128), 1), 4)
    laid = [[jnp.zeros((batches, 128), F32) for _ in range(2)] for _ in range(4)]
    for c in range(16):
        here = group_of == c % 8
        every = pl.ds(c, batches, stride=16)
        lines = drawn[every, :]
        for field in range(3):
            turn = (c - field) * DEG % 128
            line = pltpu.roll(lines, turn, 1) if turn else lines
            laid[field][c // 8] = jnp.where(here, line, laid[field][c // 8])
        laid[3][c // 8] = jnp.where(here, held_by[every, :], laid[3][c // 8])
    part_of, rest, share, keeper = [jnp.concatenate(halves, axis=1) for halves in laid]
    inside = part_of < NODES // BND
    source = jnp.where(inside, keeper, part_of - NODES // BND)
    which = keeper * BND + rest
    member_at = lax.shift_right_logical(iota((batches, 256), 1), 4).astype(F32)
    for number, values in enumerate((
        source * 16 + member_at,
        jnp.where(inside, part_of * BND + rest, -1.0),
        share,
        jnp.where(inside | (which >= 256), -1.0, which),
        jnp.where(inside | (which < 256), -1.0, which - 256),
        source,
    )):
        flat[:, number * 256 : number * 256 + 256] = values
    all_bounds = meta[:, 3 * DEG : 4 * DEG, :].reshape(GROUP * 16, NODES)
    for part in range(2):
        pick = mark(iota((GROUP, GROUP * 16), 1) == iota((GROUP, GROUP * 16), 0) * 16 + part)
        bound[part] = mm(pick, all_bounds).astype(BF16)

    def build_one(batch):
        one, nothing = jnp.ones((16, 256), BF16), jnp.zeros((16, 256), BF16)

        def line(field):
            return flat[pl.ds(batch, 1), field * 256 : field * 256 + 256]

        def tall(values):
            return jnp.broadcast_to(values, (16, 256)).astype(BF16)

        def chart(values, entry):
            strips = []
            for i in range(16):
                goal = (iota((16, 256), 0) + i * 16).astype(F32).astype(BF16)
                strips.append(jnp.where(values == goal, entry, nothing))
            return jnp.concatenate(strips, axis=0)

        far = mm(bound[0], chart(tall(line(3)), one)) + mm(bound[1], chart(tall(line(4)), one))
        far = jnp.where(iota((GROUP, 256), 0).astype(F32) == line(5), far, 0.0)
        near = line(1)
        low = jnp.where(near < 0, jnp.sum(far, axis=0, keepdims=True), near)
        mixed = nt(chart(tall(line(0)), tall(line(2))), chart(tall(low), one)).astype(BF16)
        choose[:, rows_at(SLOTS + batch * 16, 16, 16), :] = mixed.reshape(GROUP, 16, 256)

    def build(pair, carry):
        build_one(pair * 2)
        build_one(pair * 2 + 1)
        return carry

    def absorb(chips, first=False):
        blocks = [chip(d) for d in chips]
        for d in chips:
            for part in range(2):
                featc_got[d, part].wait_recv()

        def rows_of(tile, carry):
            rows = rows_at(tile * 256, 256, 256)
            product = None if first else acc[rows, :]
            for block in blocks:
                for i in range(2):
                    more = mm(choose[block * 2 + i, rows, :], table[block, i * NODES : (i + 1) * NODES, :])
                    product = more if product is None else product + more
            acc[rows, :] = product
            return carry

        lax.fori_loop(0, 2 * SLOTS // 256, rows_of, 0)

    lax.fori_loop(0, 8, build, 0)
    feat_step(2, 0)
    lax.fori_loop(8, SLOTS // 32, build, 0)
    feat_step(2, 1)
    msg_got = []
    for k in range(1, GROUP):
        to = lax.div(lax.rem(me + k, GROUP), 2)
        msg_got.append(send(msg_out.at[to], msg_in.at[me], msg_s.at[k - 1], msg_r.at[k - 1], at_shard(k)))
    absorb((0,), True)
    absorb((-1, 1))
    absorb((-2, 2))
    feat_step(3, 0)
    feat_step(3, 1)
    absorb((-3, 3))
    absorb((4,))

    local[0].wait()

    def embed(tile, carry):
        rows = rows_at(tile * 256, 256, 256)
        sums = wsum[rows, :]
        scale = 1.0 / jnp.where(sums > 0, sums, 1.0)
        itself = acc[rows, :].astype(BF16)
        around = (acc[rows_at(SLOTS + tile * 256, 256, 256), :] * wide(scale, 4)).astype(BF16)
        joined[rows, 0:WIDTH] = itself
        joined[rows, WIDTH:] = around
        projected = mm(itself, gcn[0:WIDTH, :]) + mm(around, gcn[WIDTH:, :])
        root = lax.rsqrt(jnp.mean(projected * projected, axis=-1, keepdims=True) + 1e-06)
        ready = projected * root
        unit[rows, :] = ready
        inv[rows, :] = jnp.broadcast_to(root, (256, 128))
        line = iota((256, REQS), 0) + tile * 256
        users = mm(mark(lax.shift_right_logical(line, 6) == iota((256, REQS), 1)), user[...])
        is_user = jnp.bitwise_and(iota((256, WIDTH), 0), PAD - 1) == 0
        stack[rows, :] = jnp.where(is_user, users, ready).astype(BF16)
        return carry

    lax.fori_loop(0, SLOTS // 256, embed, 0)
    stack[SLOTS : SLOTS + PAD, :] = jnp.zeros((PAD, WIDTH), BF16)

    def gram_one(q):
        grams[q] = nt(stack[rows_at(q * PAD, PAD, PAD), :], stack[rows_at(q * PAD, 2 * PAD, PAD), :]) * ROOT

    for q in range(REQS):
        gram_one(q)

    lane8 = iota((REQS, 128), 1)
    strips = [jnp.zeros((REQS, 128), F32) for _ in range(PAIRS // 128 + 2)]
    for i in range(1, CAND + 1):
        strip, shift = divmod(i * (i - 1) // 2, 128)
        line = jnp.where(lane8 < i, grams[:, i, :], 0.0)
        if shift:
            line = pltpu.roll(line, shift, 1)
        if shift + i > 128:
            strips[strip] = strips[strip] + jnp.where(lane8 >= shift, line, 0.0)
            strips[strip + 1] = strips[strip + 1] + jnp.where(lane8 < shift, line, 0.0)
        else:
            strips[strip] = strips[strip] + line
    whole = PAIRS // 128 * 128
    pairs = jnp.concatenate(strips[: PAIRS // 128], axis=1).astype(BF16)
    tail = strips[PAIRS // 128][:, 0 : PAIRS - whole].astype(BF16)

    local[1].wait()
    split = WIDTH + whole
    pre = mm(user[...], mlp[0:WIDTH, :]) + mm(pairs, mlp[WIDTH:split, :])
    pre = pre + mm(tail, mlp[split : WIDTH + PAIRS, :])
    bend = math.sqrt(2.0 / math.pi)
    curve = jnp.tanh(bend * (pre + 0.044715 * (pre * pre * pre)))
    hidden = (pre * (0.5 * (1.0 + curve))).astype(BF16)
    out_w = out_weight[...].astype(F32).reshape(1, -1)
    click_out[...] = nt(jnp.broadcast_to(out_w, (REQS, out_w.shape[1])).astype(BF16), hidden)[0]
    given_logit = jnp.zeros((REQS, 1), F32)
    for q in range(REQS):
        given_logit = jnp.where(iota((REQS, 1), 0) == q, logit_grad[q], given_logit)
    slope = 0.5 * (1.0 + curve) + 0.5 * pre * (1.0 - curve * curve) * bend * (1.0 + 3 * 0.044715 * pre * pre)
    hidden_grad = (given_logit * out_w * slope).astype(BF16)
    pair_grad[:, whole:] = jnp.zeros((REQS, 128), F32)
    pair_grad[:, 0:whole] = nt(hidden_grad, mlp[WIDTH:split, :])
    pair_grad[:, whole:PAIRS] = nt(hidden_grad, mlp[split : WIDTH + PAIRS, :])

    lower[...] = jnp.zeros((REQS, PAD, 128), F32)
    for i in range(1, CAND + 1):
        strip, shift = divmod(i * (i - 1) // 2, 128)
        line = pair_grad[:, strip * 128 : strip * 128 + 128]
        if shift:
            line = pltpu.roll(line, 128 - shift, 1)
        if shift + i > 128:
            more = pltpu.roll(pair_grad[:, strip * 128 + 128 : strip * 128 + 256], 128 - shift, 1)
            line = jnp.where(lane8 < 128 - shift, line, more)
        lower[:, i, :] = jnp.where(lane8 < i, line, 0.0)

    def back_one(q):
        under = lower[q]
        both = (under[:, 0:PAD] + under.T[0:PAD, :]).astype(BF16)
        rows = rows_at(q * PAD, PAD, PAD)
        grad = mm(both, stack[rows, :]) * ROOT
        row = iota((PAD, WIDTH), 0)
        grad = jnp.where((row >= 1) & (row <= CAND), grad, 0.0).astype(BF16)
        cand_grad[rows, :] = grad
        ready, given = unit[rows, :], grad.astype(F32)
        along = jnp.mean(ready * given, axis=-1, keepdims=True)
        pre_grad[rows, :] = (wide(inv[rows, :], 4) * (given - ready * along)).astype(BF16)

    def back(four, carry):
        for q in range(4):
            back_one(four * 4 + q)
        return carry

    lax.fori_loop(0, REQS // 4, back, 0)

    def fill(four, carry):
        picked = mm(place[rows_at(four * 256, 256, 256), :], cand_grad[...])
        for j in range(4):
            one = picked[j * 64 : j * 64 + CAP]
            both = jnp.concatenate([one[:, 0 : WIDTH // 2], one[:, WIDTH // 2 :]], axis=0)
            outbox[four * 4 + j] = both.astype(BF16)
        return carry

    lax.fori_loop(0, 4, fill, 0)
    my_box = inbox.at[rows_at(me * 2 * CAP, 2 * CAP, 16)]
    box_got = []

    def send_boxes(steps_away):
        for k in steps_away:
            to = lax.rem(me + k, GROUP)
            box_got.append(send(outbox.at[to], my_box, box_s.at[k - 1], box_r.at[k - 1], at_shard(k)))

    send_boxes((8, 7, 9, 6, 10, 1, 15, 2, 14, 3, 13))
    kept = pltpu.make_async_copy(outbox.at[me], my_box, w_sem.at[2])
    kept.start()

    def weight_term(tile, carry):
        cols = rows_at(tile * 256, 256, 256)
        term[cols, :] = tn(joined[:, cols], pre_grad[...])
        return carry

    lax.fori_loop(0, 4, weight_term, 0)

    rows, width = term.shape
    chunk = width // CHUNKS
    in_flight = {}

    def pass_on(c, number, src, dst, peer):
        in_flight[c, number] = send(src, dst, red_s.at[c, number], red_r.at[c, number], peer)

    def arrive(c, numbers):
        for number in numbers:
            in_flight[c, number].wait_recv()

    def step0(c):
        theirs = pl.multiple_of((1 - core) * (rows // 2), rows // 2)
        send0[c] = term[pl.ds(theirs, rows // 2), c * chunk : (c + 1) * chunk].astype(BF16)
        pass_on(c, 0, send0.at[c], recv0.at[c], other_core)

    def step1(c):
        arrive(c, [0])
        mine = pl.multiple_of(core * (rows // 2), rows // 2)
        total = term[pl.ds(mine, rows // 2), c * chunk : (c + 1) * chunk] + recv0[c].astype(F32)
        half[c] = total.reshape(N_X, rows // 8, chunk)
        send1[c] = total.astype(BF16).reshape(N_X, rows // 8, chunk)
        for k in range(1, N_X):
            to = lax.rem(x + k, N_X)
            pass_on(c, k, send1.at[c, to], recv1.at[c, k - 1], at_x(k))

    def step2(c):
        arrive(c, range(1, 4))
        total = half[c, x]
        for k in range(N_X - 1):
            total = total + recv1[c, k].astype(F32)
        for j in range(chunk // 128):
            tiles = total[:, j * 128 : j * 128 + 128].reshape(8, 16, 128)
            tiled[c, j * 8 : j * 8 + 8] = tiles
            send2[c, j * 8 : j * 8 + 8] = tiles.astype(BF16)
        tiled[c, 16:24] = jnp.zeros((8, 16, 128), F32)
        send2[c, 16:24] = jnp.zeros((8, 16, 128), BF16)
        for k in range(1, N_Z):
            to = lax.rem(z + k, N_Z)
            pass_on(c, 3 + k, send2.at[c, pl.ds(to * 2, 2)], recv2.at[c, k - 1], at_z(k))

    def step3(c):
        arrive(c, range(4, 15))
        total = tiled[c, pl.ds(z * 2, 2)]
        for k in range(N_Z - 1):
            total = total + recv2[c, k].astype(F32)
        slots3[c, y] = total.astype(BF16)
        for k in range(1, N_Y):
            pass_on(c, 14 + k, slots3.at[c, y], slots3.at[c, y], at_y(k))

    def step4(c):
        arrive(c, range(15, 22))
        total = slots3[c, 0].astype(F32)
        for k in range(1, N_Y):
            total = total + slots3[c, k].astype(F32)
        fin4[c, z] = (total * (1.0 / (GROUP * N_X * N_Z))).astype(BF16)
        for k in range(1, N_Z):
            pass_on(c, 21 + k, fin4.at[c, z], fin4.at[c, z], at_z(k))

    def step5(c):
        arrive(c, range(22, 33))
        fin5[c, x] = fin4[c].reshape(24, 16, 128)[0:16]
        for k in range(1, N_X):
            pass_on(c, 32 + k, fin5.at[c, x], fin5.at[c, x], at_x(k))

    def step6(c):
        arrive(c, range(33, 36))
        fin6[c, core] = fin5[c]
        pass_on(c, 36, fin6.at[c, core], fin6.at[c, core], other_core)

    def step7(c):
        arrive(c, [36])
        for j in range(chunk // 128):
            done = fin6[c, :, :, j * 8 : j * 8 + 8].reshape(rows, 128)
            mean_out[:, c * chunk + j * 128 : c * chunk + j * 128 + 128] = done

    steps = (step0, step1, step2, step3, step4, step5, step6, step7)
    waves = [
        [(wave - c, c) for c in range(CHUNKS) if 0 <= wave - c < len(steps)]
        for wave in range(len(steps) + CHUNKS - 1)
    ]

    def run(wave):
        for step, c in waves[wave]:
            steps[step](c)

    run(0)
    run(1)
    lax.fori_loop(SLOTS // 32, LINES // 32, build, 0)
    run(2)

    def own_part(p, total):
        block = table[lax.div(p, 2), rows_at(lax.rem(p, 2) * NODES, NODES, NODES), :]
        return total + mm(choose[p, 2 * SLOTS :, :], block)

    shares = lax.fori_loop(0, GROUP, own_part, jnp.zeros((NODES, WIDTH), F32))
    around = (shares * wide(1.0 / wsum[SLOTS:, :], 4)).astype(BF16)
    projected = mm(feats[...], gcn[0:WIDTH, :]) + mm(around, gcn[WIDTH:, :])
    root = lax.rsqrt(jnp.mean(projected * projected, axis=-1, keepdims=True) + 1e-06)
    emb_out[...] = (projected * root).astype(BF16)
    run(3)

    for copy in msg_got:
        copy.wait_recv()
    box_rows = GROUP * 2 * CAP
    lane16 = iota((16, 128), 1)
    marks = [jnp.zeros((16, 128), F32) for _ in range(box_rows // 128 + 1)]
    for p in range(GROUP):
        strip, shift = divmod(p * 2 * CAP, 128)
        line = msg_in[p].astype(F32)
        line = jnp.where(core == 1, pltpu.roll(line, 64, 1), line)
        line = jnp.where(lane16 < CAP, line, 0.0)
        line = line + pltpu.roll(line, CAP, 1)
        if shift:
            line = pltpu.roll(line, shift, 1)
        if shift + 2 * CAP > 128:
            marks[strip] = marks[strip] + jnp.where(lane16 >= shift, line, 0.0)
            marks[strip + 1] = marks[strip + 1] + jnp.where(lane16 < shift, line, 0.0)
        else:
            marks[strip] = marks[strip] + line
    run(4)
    send_boxes((4, 12, 5, 11))
    for strip in range(box_rows // 128):
        line = lax.rem(iota((1, 128), 1) + strip * 128, 2 * CAP)
        goal = marks[strip][0:1, :]
        cols = slice(strip * 128, strip * 128 + 128)
        here = iota((NODES, 128), 0).astype(F32)
        spread[0:NODES, cols] = mark(here == jnp.where(line < CAP, goal, -1.0))
        spread[NODES:, cols] = mark(here == jnp.where(line < CAP, -1.0, goal))
    for wave in range(5, len(waves)):
        run(wave)

    for copy in box_got:
        copy.wait_recv()
    kept.wait()
    for part in range(2):
        cols = slice(part * NODES, part * NODES + NODES)
        grad_out[:, cols] = mm(spread[cols, :], inbox[...])
    for copy in sent:
        copy.wait_send()


def on_device(
    node_feats,
    send_rows,
    neighbors,
    neighbor_weight,
    gcn_weight,
    user_dense,
    cand_owner,
    cand_row,
    mlp_weight,
    out_weight,
    logit_grad,
):
    rows, width = gcn_weight.shape
    chunk = width // CHUNKS
    eighth = rows // 8
    vmem = pl.BlockSpec(memory_space=pltpu.VMEM)
    hbm = pl.BlockSpec(memory_space=pl.ANY)
    smem = pl.BlockSpec(memory_space=pltpu.SMEM)
    dma = pltpu.SemaphoreType.DMA
    embeddings, embed_grad, clicks, mean = pl.pallas_call(
        kernel,
        out_shape=(
            jax.ShapeDtypeStruct((NODES, WIDTH), BF16),
            jax.ShapeDtypeStruct((NODES, WIDTH), F32),
            jax.ShapeDtypeStruct((REQS,), F32),
            jax.ShapeDtypeStruct((rows, width), BF16),
        ),
        in_specs=[vmem, vmem, vmem, vmem, hbm, vmem, vmem, vmem, hbm, vmem, smem],
        out_specs=(vmem, vmem, vmem, vmem),
        scratch_shapes=[
            pltpu.VMEM((4 * DEG, NODES), F32),
            pltpu.VMEM((GROUP, 4 * DEG, NODES), BF16),
            pltpu.VMEM((N_Y, 2 * NODES, WIDTH), BF16),
            pltpu.VMEM((GROUP * 64, SLOTS), BF16),
            pltpu.VMEM((GROUP // 2, 16, 128), BF16),
            pltpu.VMEM((GROUP, 16, 128), BF16),
            pltpu.VMEM((GROUP, SLOTS + LINES, NODES), BF16),
            pltpu.VMEM((LINES, 128), F32),
            pltpu.VMEM((LINES, 128), F32),
            pltpu.VMEM((LINES // 16, 6 * 256), F32),
            pltpu.VMEM((2, GROUP, NODES), BF16),
            pltpu.VMEM((LINES, 128), F32),
            pltpu.VMEM((2 * SLOTS, WIDTH), F32),
            pltpu.VMEM((SLOTS, 2 * WIDTH), BF16),
            pltpu.VMEM((SLOTS, WIDTH), F32),
            pltpu.VMEM((SLOTS, 128), F32),
            pltpu.VMEM((SLOTS + PAD, WIDTH), BF16),
            pltpu.VMEM((REQS, PAD, 128), F32),
            pltpu.VMEM((REQS, PAD, 128), F32),
            pltpu.VMEM((REQS, PAIRS // 128 * 128 + 128), F32),
            pltpu.VMEM((SLOTS, WIDTH), BF16),
            pltpu.VMEM((SLOTS, WIDTH), BF16),
            pltpu.VMEM((rows, width), F32),
            pltpu.VMEM((GROUP, 2 * CAP, WIDTH // 2), BF16),
            pltpu.VMEM((GROUP * 2 * CAP, WIDTH // 2), BF16),
            pltpu.VMEM((2 * NODES, GROUP * 2 * CAP), BF16),
            pltpu.VMEM(mlp_weight.shape, BF16),
            pltpu.VMEM((rows, width), BF16),
            pltpu.VMEM((CHUNKS, rows // 2, chunk), BF16),
            pltpu.VMEM((CHUNKS, rows // 2, chunk), BF16),
            pltpu.VMEM((CHUNKS, N_X, eighth, chunk), F32),
            pltpu.VMEM((CHUNKS, N_X, eighth, chunk), BF16),
            pltpu.VMEM((CHUNKS, N_X - 1, eighth, chunk), BF16),
            pltpu.VMEM((CHUNKS, 24, 16, 128), F32),
            pltpu.VMEM((CHUNKS, 24, 16, 128), BF16),
            pltpu.VMEM((CHUNKS, N_Z - 1, 2, 16, 128), BF16),
            pltpu.VMEM((CHUNKS, N_Y, 2, 16, 128), BF16),
            pltpu.VMEM((CHUNKS, N_Z, 2, 16, 128), BF16),
            pltpu.VMEM((CHUNKS, N_X, 16, 16, 128), BF16),
            pltpu.VMEM((CHUNKS, 2, N_X, 16, 16, 128), BF16),
            dma((3,)),
            dma((8,)),
            dma((8,)),
            dma((8,)),
            dma((8,)),
            dma((16,)),
            dma((16,)),
            dma((16,)),
            dma((16,)),
            dma((GROUP - 1,)),
            dma((GROUP - 1,)),
            dma((GROUP - 1,)),
            dma((GROUP - 1,)),
            dma((CHUNKS, 37)),
            dma((CHUNKS, 37)),
        ],
        compiler_params=pltpu.CompilerParams(
            collective_id=0, has_side_effects=True, vmem_limit_bytes=58 * 1024 * 1024
        ),
    )(
        node_feats,
        send_rows,
        neighbors.T,
        neighbor_weight.T,
        gcn_weight,
        user_dense,
        cand_owner.reshape(REQS, CAND),
        cand_row,
        mlp_weight,
        out_weight,
        logit_grad,
    )
    return (embeddings, embed_grad, clicks, mean.astype(F32))


def solution(mesh):
    return jax.shard_map(
        on_device,
        mesh=mesh,
        in_specs=(
            P(("shard", "rep"), None),
            P(("shard", "rep"), None, None),
            P(("shard", "rep"), None),
            P(("shard", "rep"), None),
            P(),
            P(("shard", "rep"), None),
            P(("shard", "rep"), None, None),
            P(("shard", "rep"), None),
            P(),
            P(),
            P(("shard", "rep")),
        ),
        out_specs=(P(("shard", "rep"), None), P(("shard", "rep"), None), P(("shard", "rep")), P()),
        check_vma=False,
    )
```
